256 devices in a mesh: group: 2 (over core), row: 4 (over z_hi), col: 32 (over z_lo, y, x).
Axes of the slice: x: 4, y: 4, z: 8 (z_hi: 4, z_lo: 2; z = z_hi * 2 + z_lo), core: 2. Of those that a mesh axis runs over, the one named last changes fastest.
Arguments:
- teacher_tokens: bfloat16 [2048, 4, 8, 1536], P(('group', 'col'), None, None, 'row'), may hold values from -6 to 6
- view_index: int32 [2048, 4], P(('group', 'col')), may hold values from 0 to 31
- aug_embed: bfloat16 [32, 1536], P(None, 'row'), may hold values from -3 to 3
- norm_gain: bfloat16 [1536], replicated, may hold values from 0.099609375 to 1.8984375
- layer_scale: bfloat16 [1536], P('row'), may hold values from 0.29882812 to 1.5
- gate_weight: bfloat16 [1536, 4096], P('col', 'row'), may hold values from -0.15625 to 0.15625
- up_weight: bfloat16 [1536, 4096], P('col', 'row'), may hold values from -0.15625 to 0.15625
- down_weight: bfloat16 [4096, 1536], P(('row', 'col')), may hold values from -0.09375 to 0.09375
- student_tokens: bfloat16 [2048, 6144], P(('group', 'col'), 'row'), may hold values from -6 to 6
- head_weight: bfloat16 [768, 1536], P(None, 'row'), may hold values from -0.21875 to 0.21875
- owner: int32 [2048, 1], P(('group', 'col')), may hold values from 0 to 31; in each aligned block of 32 rows (0 to 31, 32 to 63, ...) at most 2 rows name the same one
Outputs:
- head_grad: float32 [768, 1536], P(None, 'row')
- owner_loss: float32 [64], P(('group', 'col'))
The draws below stay inside these ranges and needn't reach their ends.
Inputs may be any that keep to these rules, and one draw needn't show every extreme that they name: Among the 32 images of one device (aligned blocks) no owner is named more than 2 times, a bound that some block reaches.
All inputs are finite; a program needn't handle non-finite values.
Results may differ from the reference program's by a relative error of at most 0.012.
Values may be sent and summed in bfloat16 or wider, within the bound.
No kernel may reach another device: no remote copies, remote signals or barrier semaphores. Data moves between devices by JAX's collectives and lax.ppermute only.
A program may use at most 64 MiB of HBM per device.

```python
import math
import jax
import jax.numpy as jnp
import numpy as np
from jax import lax

D = 1536
FF = 4096
SW = 768
IMG_DEV = 32
VIEWS = 4
PATCH = 8
AUGS = 32
IMAGES = 2048
MOST = 2
N_GROUP = 2
N_COL = 32


def set_ends(values, own_key, low, largest):
    shape = values.shape
    place = [jax.random.randint(jax.random.fold_in(own_key, axis), (), 0, shape[axis]) for axis in range(len(shape))]
    values = values.at[tuple(place)].set(low)
    longest = shape.index(max(shape))
    place[longest] = (place[longest] + 1) % shape[longest]
    return values.at[tuple(place)].set(largest)


def levels(stream_key, shape, cuts, smallest, high):
    def one(position, blocks):
        heights = jax.random.uniform(jax.random.fold_in(jax.random.fold_in(stream_key, 6), position), (blocks,), jnp.float32, smallest / len(cuts), high / len(cuts))
        return jnp.repeat(jnp.exp(heights), shape[position] // blocks).reshape((-1,) + (1,) * (len(shape) - position - 1))

    level = one(*cuts[0])
    for cut in cuts[1:]:
        level = level * one(*cut)
    return level


def assign_block(rng, own, number, rows, count, top, reach, skew):
    ranking = jax.random.permutation(rng, count)
    packed, ordinary = load_shares(count, rows * top, reach, skew, True), load_shares(count, rows * top, reach, skew, False)
    places = jnp.arange(count)

    def named(tallies, rotation):
        used = int((tallies > 0).sum())
        fixed = max(1, used // 4)
        moved = fixed + (places - fixed + rotation * (used - fixed)) % max(1, count - fixed)
        return jnp.zeros((count,), jnp.int32).at[ranking[jnp.where(places < fixed, places, moved)]].set(jnp.asarray(tallies, jnp.int32))

    tallies = jnp.where(number % 4 == 0, named(packed, number // 4), named(ordinary, number - number // 4 - 1))
    mixed = jax.random.permutation(jax.random.fold_in(own, 3), count)
    source_of, sink = mixed[0:count // 2 * 2:2], mixed[1:count // 2 * 2:2]
    room = jnp.minimum(tallies[source_of] - 1, reach - tallies[sink]) // 2
    room = jnp.where((source_of == ranking[0]) | (sink == ranking[0]) | (tallies[sink] == 0), 0, jnp.maximum(room, 0))
    moved = jax.random.randint(jax.random.fold_in(own, 4), (count // 2,), 0, 1 << 20) % (room + 1)
    tallies = tallies.at[source_of].add(-moved).at[sink].add(moved)
    members = jnp.searchsorted(jnp.cumsum(tallies), jnp.arange(rows * top), side="right").astype(jnp.int32)
    listing = members.reshape(top, rows).T
    listing = listing[jax.random.permutation(jax.random.fold_in(own, 1), rows)]
    rotation = jax.random.randint(jax.random.fold_in(own, 2), (rows, 1), 0, top)
    return jnp.take_along_axis(listing, (jnp.arange(top)[None, :] + rotation) % top, axis=1)


def load_shares(count, total, bound, slope, full):
    portions = [(1 << 20) // math.isqrt(standing ** slope) + 1 for standing in range(1, count + 1)]
    largest = bound if full else min(bound, max(-(-total // count), total * portions[0] // sum(portions)))
    least = 1 if total - largest >= count - 1 else 0
    given, surplus = [largest] + [least] * (count - 1), total - largest - least * (count - 1)
    while surplus > 0:
        movable = [i for i in range(1, count) if given[i] < largest] or [i for i in range(1, count) if given[i] < bound]
        pool, remaining = sum([portions[i] for i in movable]), surplus
        for i in movable:
            addition = min(bound - given[i], max(1, remaining * portions[i] // pool), surplus)
            given[i] = given[i] + addition
            surplus = surplus - addition
    return np.array(given)


def scatter_about(rng, shape, scale, bound, cuts=(), kind=jnp.bfloat16):
    result = scale * jax.random.normal(rng, shape, jnp.float32)
    if cuts:
        result = result * levels(rng, shape, cuts, -0.22, 0.18)
    return jnp.clip(result, -bound, bound).astype(kind)


def setup_inputs(seed: int = 0) -> dict:
    streams_of = jax.random.split(jax.random.key(seed), 12)
    teacher_tokens = scatter_about(streams_of[0], (IMAGES, VIEWS, PATCH, D), 1.0, 6.0, ((0, 64), (3, 4)))
    view_index = set_ends(jax.random.randint(streams_of[1], (IMAGES, VIEWS), 0, AUGS), jax.random.fold_in(streams_of[1], 1), 0, AUGS - 1).astype(jnp.int32)
    aug_embed = scatter_about(streams_of[2], (AUGS, D), 0.5, 3.0, ((1, 4),))
    norm_gain = jnp.clip(1.0 + 0.18 * jax.random.normal(streams_of[3], (D,), jnp.float32), 0.099609375, 1.8984375).astype(jnp.bfloat16)
    layer_scale = jnp.clip(jnp.exp(math.log(1.5) - 1.6133518 * jax.random.uniform(streams_of[4], (D,), jnp.float32) ** levels(streams_of[4], (D,), ((0, 4),), -0.2, 0.2)), 0.29882812, 1.5).astype(jnp.bfloat16)
    gate_weight = scatter_about(streams_of[5], (D, FF), D ** -0.5, 0.15625, ((0, 32), (1, 4)))
    up_weight = scatter_about(streams_of[6], (D, FF), D ** -0.5, 0.15625, ((0, 32), (1, 4)))
    down_weight = scatter_about(streams_of[7], (FF, D), FF ** -0.5, 0.09375, ((0, 128),))
    student_tokens = scatter_about(streams_of[8], (IMAGES, PATCH * SW), 1.0, 6.0, ((0, 64), (1, 4)))
    head_weight = scatter_about(streams_of[9], (SW, D), SW ** -0.5, 0.21875, ((1, 4),))
    owner_keys = jax.random.split(jax.random.fold_in(streams_of[10], 1), IMAGES // IMG_DEV)
    owner_turns = jax.random.permutation(jax.random.fold_in(streams_of[10], 3), IMAGES // IMG_DEV)
    owner = jax.vmap(lambda own, number: assign_block(jax.random.fold_in(streams_of[10], 2), own, number, IMG_DEV, N_COL, 1, MOST, 2))(owner_keys, owner_turns).reshape((IMAGES, 1))
    return dict(teacher_tokens=teacher_tokens, view_index=view_index, aug_embed=aug_embed, norm_gain=norm_gain, layer_scale=layer_scale, gate_weight=gate_weight, up_weight=up_weight, down_weight=down_weight, student_tokens=student_tokens, head_weight=head_weight, owner=owner)


def reference(teacher_tokens, view_index, aug_embed, norm_gain, layer_scale, gate_weight, up_weight, down_weight, student_tokens, head_weight, owner):
    blocks = IMAGES // IMG_DEV

    def teach(pieces):
        tokens_blk, index_blk = pieces
        shifted = (tokens_blk.astype(jnp.float32) + aug_embed[index_blk].astype(jnp.float32)[:, :, None, :]).astype(jnp.bfloat16)
        flat = shifted.reshape(-1, D).astype(jnp.float32)
        center = flat - lax.optimization_barrier(jnp.mean(flat, axis=1, keepdims=True))
        spread = lax.optimization_barrier(jnp.mean(center * center, axis=1, keepdims=True))
        normed = (center * lax.rsqrt(spread + 1e-06) * norm_gain.astype(jnp.float32)).astype(jnp.bfloat16)
        gate = jnp.dot(normed, gate_weight, preferred_element_type=jnp.float32)
        upward = jnp.dot(normed, up_weight, preferred_element_type=jnp.float32)
        hidden = (jax.nn.silu(gate) * upward).astype(jnp.bfloat16)
        branch = jnp.dot(hidden, down_weight, preferred_element_type=jnp.float32).reshape(IMG_DEV, VIEWS, PATCH, D)
        target = lax.optimization_barrier(jnp.mean(shifted.astype(jnp.float32), axis=1)) + layer_scale.astype(jnp.float32) * lax.optimization_barrier(jnp.mean(branch, axis=1))
        return target.astype(jnp.bfloat16)
    targets = lax.map(teach, (teacher_tokens.reshape(blocks, IMG_DEV, VIEWS, PATCH, D), view_index.reshape(blocks, IMG_DEV, VIEWS)))
    pupils = student_tokens.reshape(blocks, IMG_DEV * PATCH, SW)

    def learn(total, pieces):
        target, pupil = pieces
        head = jnp.dot(pupil, head_weight, preferred_element_type=jnp.float32)
        middle = lax.optimization_barrier(jnp.mean(head, axis=1, keepdims=True))
        spread = lax.optimization_barrier(jnp.mean(head * head, axis=1, keepdims=True)) - middle * middle
        scaler = lax.rsqrt(spread + 1e-05)
        pred = (head - middle) * scaler
        diff = pred - target.reshape(-1, D).astype(jnp.float32)
        errors = lax.optimization_barrier(jnp.sum((diff * diff).reshape(IMG_DEV, PATCH * D), axis=1)) / (PATCH * D)
        dpred = 2.0 * diff / IMAGES
        first = lax.optimization_barrier(jnp.mean(dpred, axis=1, keepdims=True))
        second = lax.optimization_barrier(jnp.mean(dpred * pred, axis=1, keepdims=True))
        dz_value = (scaler * (dpred - first - pred * second)).astype(jnp.bfloat16)
        total = total + lax.dot_general(pupil, dz_value, (((0,), (0,)), ((), ())), preferred_element_type=jnp.float32)
        return (total, errors)
    head_grad, errors = lax.scan(learn, jnp.zeros((SW, D), jnp.float32), (targets, pupils))
    groups = (jnp.arange(blocks, dtype=jnp.int32) // N_COL)[:, None] * N_COL
    segment = (groups + owner.reshape(blocks, IMG_DEV)).reshape(-1)
    owner_loss = jax.ops.segment_sum(errors.reshape(-1), segment, num_segments=N_GROUP * N_COL)
    return (head_grad, owner_loss)
```

```python
import jax
import jax.numpy as jnp
from jax import lax
from jax.sharding import Mesh, PartitionSpec as P

D = 1536
SW = 768
ROWS = 4
YX = ("y", "x")
COL = ("zl", "y", "x")
EVERY = ("group", "zl", "y", "x")
IMAGES = 2048


def shift(value, axis, size, by):
    return lax.ppermute(value, axis, [(i, (i + by) % size) for i in range(size)])


def middle(pieces, gate_halves, up_halves, down_halves, norm_gain, row, group):
    tokens = jnp.concatenate(pieces, axis=1).astype(jnp.float32)
    center = tokens - jnp.mean(tokens, axis=1, keepdims=True)
    spread = jnp.mean(center * center, axis=1, keepdims=True)
    normed = center * lax.rsqrt(spread + 1e-06)
    normed = jnp.stack([normed[:, 384 * j : 384 * j + 384] for j in range(4)])
    normed = jnp.take(normed, (jnp.arange(4) - row) % 4, axis=0)
    normed = jnp.concatenate([normed[j] for j in range(4)], axis=1)
    normed = (normed * norm_gain.astype(jnp.float32)).astype(jnp.bfloat16)

    def whole(halves):
        own, other = halves
        low = jnp.where(group == 0, own, other)
        high = jnp.where(group == 0, other, own)
        return jnp.concatenate([low, high], axis=0)

    gate = jnp.dot(normed, whole(gate_halves), preferred_element_type=jnp.float32)
    upward = jnp.dot(normed, whole(up_halves), preferred_element_type=jnp.float32)
    hidden = jax.nn.silu(gate) * upward
    hidden = jnp.mean(hidden.reshape(32, 4, 8, 1024), axis=1).reshape(256, 1024).astype(jnp.bfloat16)
    branch = jnp.dot(hidden, whole(down_halves), preferred_element_type=jnp.float32)
    parts = jnp.stack([branch[:, 384 * j : 384 * j + 384] for j in range(4)])
    parts = jnp.take(parts, (jnp.arange(4) + row) % 4, axis=0)
    return parts


def shards(
    teacher_tokens,
    view_index,
    aug_embed,
    norm_gain,
    layer_scale,
    gate_weight,
    up_weight,
    down_weight,
    student_tokens,
    head_weight,
    owner,
):
    group, row, zl = lax.axis_index("group"), lax.axis_index("row"), lax.axis_index("zl")
    images = teacher_tokens.shape[0]

    def fetch(block):
        other = lax.ppermute(block, ("group", "zl"), [(0, 1), (3, 2)])
        mine = jnp.where(group == zl, block, other)
        spread = jnp.broadcast_to(mine[None], (16,) + mine.shape)
        return lax.all_to_all(spread, YX, 0, 0, tiled=True)

    gate_up = fetch(jnp.stack([gate_weight, up_weight]))
    gate_own = gate_up[:, 0].reshape(768, 1024)
    up_own = gate_up[:, 1].reshape(768, 1024)
    down_own = fetch(down_weight).reshape(512, D)
    gate_other = shift(gate_own, "group", 2, 1)
    up_other = shift(up_own, "group", 2, 1)
    down_other = shift(down_own, "group", 2, 1)

    kinds = aug_embed.shape[0]
    kind_table = (
        view_index.reshape(-1)[:, None] == jnp.arange(kinds, dtype=jnp.int32)[None, :]
    ).astype(jnp.bfloat16)
    embedded = jnp.dot(kind_table, aug_embed, preferred_element_type=jnp.float32).reshape(
        images, 4, 1, 384
    )
    shifted = (teacher_tokens.astype(jnp.float32) + embedded).astype(jnp.bfloat16)
    own = shifted.reshape(1024, 384)
    before = shift(own, "row", 4, 1)
    after = shift(own, "row", 4, -1)
    far_top = shift(before[:512], "row", 4, 1)
    far_bottom = shift(after[512:], "row", 4, -1)
    far = jnp.concatenate([far_top, far_bottom], axis=0)
    residual = jnp.mean(shifted.astype(jnp.float32), axis=1).reshape(256, 384)

    pupils = [student_tokens] + [shift(student_tokens, "row", 4, -j) for j in (1, 2, 3)]
    pupils = jnp.stack(pupils).reshape(4, images, 2, SW)
    pupils = jnp.take(pupils, (jnp.arange(4) - row) % 4, axis=0)
    pupils = pupils.transpose(1, 0, 2, 3).reshape(256, SW)
    head = jnp.dot(pupils, head_weight, preferred_element_type=jnp.float32)
    sums = lax.psum(jnp.stack([jnp.sum(head, axis=1), jnp.sum(head * head, axis=1)]), "row")
    center = (sums[0] / D)[:, None]
    scaler = lax.rsqrt((sums[1] / D)[:, None] - center * center + 1e-05)
    pred = (head - center) * scaler

    parts = middle(
        (own, after, far, before),
        (gate_own, gate_other),
        (up_own, up_other),
        (down_own, down_other),
        norm_gain,
        row,
        group,
    )
    narrow = parts.astype(jnp.bfloat16)
    got = [shift(narrow[j], "row", 4, j) for j in (2, 1, 3)]
    averaged = parts[0] + got[0].astype(jnp.float32) + got[1].astype(jnp.float32) + got[2].astype(jnp.float32)
    target = (residual + layer_scale.astype(jnp.float32) * averaged).astype(jnp.bfloat16)
    diff = pred - target.astype(jnp.float32)
    dpred = 2.0 * diff / IMAGES
    totals = lax.psum(
        jnp.stack(
            [jnp.sum(dpred, axis=1), jnp.sum(dpred * pred, axis=1), jnp.sum(diff * diff, axis=1)]
        ),
        "row",
    )
    dz = (
        scaler * (dpred - (totals[0] / D)[:, None] - pred * (totals[1] / D)[:, None])
    ).astype(jnp.bfloat16)
    errors = jnp.sum(totals[2].reshape(images, 8), axis=1) / (8 * D)
    mine = owner == jnp.arange(32, dtype=jnp.int32)[None, :]
    loss = jnp.sum(jnp.where(mine, errors[:, None], 0.0), axis=0)
    loss_high = loss.astype(jnp.bfloat16)
    loss_low = (loss - loss_high.astype(jnp.float32)).astype(jnp.bfloat16)

    grad = lax.dot_general(pupils, dz, (((0,), (0,)), ((), ())), preferred_element_type=jnp.float32)
    grad = grad.reshape(2, 384, 384)
    keep = lax.dynamic_index_in_dim(grad, group, 0, keepdims=False)
    give = lax.dynamic_index_in_dim(grad, 1 - group, 0, keepdims=False)
    half = keep + shift(give.astype(jnp.bfloat16), "group", 2, 1).astype(jnp.float32)
    half = half.astype(jnp.bfloat16).reshape(32, 12, 384)
    note = jnp.stack([loss_high, loss_low], axis=1)[:, :, None]
    note = jnp.broadcast_to(note, (32, 2, 384))
    packet = jnp.concatenate([half, note], axis=1)
    packet = lax.all_to_all(packet, COL, 0, 0, tiled=True).astype(jnp.float32)
    summed = jnp.sum(packet, axis=0)
    owner_loss = (summed[12, :1] + summed[13, :1])
    part = summed[:12].astype(jnp.bfloat16)
    part = lax.all_to_all(jnp.broadcast_to(part[None], (32, 12, 384)), COL, 0, 0, tiled=True)
    part = part.reshape(384, 384)
    twin = shift(part, "group", 2, 1)
    head_grad = jnp.concatenate(
        [jnp.where(group == 0, part, twin), jnp.where(group == 0, twin, part)], axis=0
    ).astype(jnp.float32)
    return (head_grad, owner_loss)


def solution(mesh):
    fine = Mesh(mesh.devices.reshape(2, 4, 2, 4, 4), ("group", "row", "zl", "y", "x"))
    return jax.shard_map(
        shards,
        mesh=fine,
        in_specs=(
            P(EVERY, None, None, "row"),
            P(EVERY, None),
            P(None, "row"),
            P(),
            P("row"),
            P(COL, "row"),
            P(COL, "row"),
            P(("row",) + COL, None),
            P(EVERY, "row"),
            P(None, "row"),
            P(EVERY, None),
        ),
        out_specs=(P(None, "row"), P(EVERY)),
        check_vma=False,
    )
```

```python
import jax
import jax.numpy as jnp
from jax import lax
from jax.experimental import pallas as pl
from jax.experimental.pallas import tpu as pltpu
from jax.sharding import Mesh, PartitionSpec as P

D = 1536
SW = 768
PART = 384
YX = ("y", "x")
COL = ("zl", "y", "x")
EVERY = ("group", "zl", "y", "x")
IMAGES = 2048
MIB = 1024 * 1024


def shift(value, axis, size, by):
    return lax.ppermute(value, axis, [(i, (i + by) % size) for i in range(size)])


def norm_kernel(place, own, after, before, far_top, far_bottom, gain, out):
    row, group = place[0], place[1]
    far = jnp.where(pl.program_id(0) < 2, far_top[...], far_bottom[...])
    pieces = [own[0], after[0], far, before[0]]
    pieces = [piece.astype(jnp.float32) for piece in pieces]
    total = sum(jnp.sum(piece, axis=1, keepdims=True) for piece in pieces)
    mean = total * (1.0 / D)
    pieces = [piece - mean for piece in pieces]
    square = sum(jnp.sum(piece * piece, axis=1, keepdims=True) for piece in pieces)
    scale = lax.rsqrt(square * (1.0 / D) + 1e-06)
    for j, piece in enumerate(pieces):
        block = lax.rem(row + j, 4)
        source = pl.multiple_of(block * PART, PART)
        target = pl.multiple_of(lax.rem(block + 2 * group, 4) * PART, PART)
        value = piece * scale * gain[:, pl.ds(source, PART)]
        out[:, pl.ds(target, PART)] = value.astype(jnp.bfloat16)


def norm(place, own, after, before, far_top, far_bottom, gain):
    piece = pl.BlockSpec((1, 256, PART), lambda b: (b // 2, b % 2, 0))
    return pl.pallas_call(
        norm_kernel,
        grid=(4,),
        in_specs=[
            pl.BlockSpec(memory_space=pltpu.SMEM),
            piece,
            piece,
            piece,
            pl.BlockSpec((256, PART), lambda b: (jnp.minimum(b, 1), 0)),
            pl.BlockSpec((256, PART), lambda b: (jnp.maximum(b - 2, 0), 0)),
            pl.BlockSpec((1, D), lambda b: (0, 0)),
        ],
        out_specs=pl.BlockSpec((256, D), lambda b: (b, 0)),
        out_shape=jax.ShapeDtypeStruct((1024, D), jnp.bfloat16),
        compiler_params=pltpu.CompilerParams(vmem_limit_bytes=24 * MIB),
        cost_estimate=pl.CostEstimate(
            flops=16 * 1024 * D, bytes_accessed=4 * 1024 * D, transcendentals=0
        ),
    )(place, own, after, before, far_top, far_bottom, gain)


def hidden_kernel(place, normed, own, other, out, weights, sems):
    group = place[1]

    def copy(side, kind, n):
        source = own if side == 0 else other
        start = pl.multiple_of(kind * 1024 + n * 256, 256)
        return pltpu.make_async_copy(
            source.at[:, pl.ds(start, 256)], weights.at[n, kind, side], sems.at[n, kind, side]
        )

    for n in range(4):
        for kind in (0, 1):
            for side in (0, 1):
                copy(side, kind, n).start()

    def step(n, carry):
        values = []
        for kind in (0, 1):
            for side in (0, 1):
                copy(side, kind, n).wait()
            values.append(
                jnp.dot(
                    normed[:, :768], weights[n, kind, 0], preferred_element_type=jnp.float32
                )
                + jnp.dot(
                    normed[:, 768:], weights[n, kind, 1], preferred_element_type=jnp.float32
                )
            )
        gate, upward = values
        hidden = gate * upward / (1.0 + jnp.exp(-gate))
        hidden = jnp.sum(hidden.reshape(32, 4, 8, 256), axis=1).reshape(256, 256) * 0.25
        target = pl.multiple_of(lax.rem(n + 2 * group, 4) * 256, 256)
        out[:, pl.ds(target, 256)] = hidden.astype(jnp.bfloat16)
        return carry

    lax.fori_loop(0, 4, step, 0)


def hidden_mean(place, normed, own, other):
    return pl.pallas_call(
        hidden_kernel,
        in_specs=[
            pl.BlockSpec(memory_space=pltpu.SMEM),
            pl.BlockSpec(memory_space=pltpu.VMEM),
            pl.BlockSpec(memory_space=pl.ANY),
            pl.BlockSpec(memory_space=pl.ANY),
        ],
        out_specs=pl.BlockSpec(memory_space=pltpu.VMEM),
        out_shape=jax.ShapeDtypeStruct((256, 1024), jnp.bfloat16),
        scratch_shapes=[
            pltpu.VMEM((4, 2, 2, 768, 256), jnp.bfloat16),
            pltpu.SemaphoreType.DMA((4, 2, 2)),
        ],
        compiler_params=pltpu.CompilerParams(vmem_limit_bytes=32 * MIB),
        cost_estimate=pl.CostEstimate(
            flops=2 * 1024 * D * 2048, bytes_accessed=10 * MIB, transcendentals=1024 * 1024
        ),
    )(place, normed, own, other)


def branch_kernel(place, hidden, own, other, out0, out1, out2, out3, weights, sems):
    row = place[0]
    outs = (out0, out1, out2, out3)

    def copy(side, j):
        source = own if side == 0 else other
        start = pl.multiple_of(lax.rem(row + j, 4) * PART, PART)
        return pltpu.make_async_copy(
            source.at[:, pl.ds(start, PART)], weights.at[j, side], sems.at[j, side]
        )

    for j in (2, 1, 3, 0):
        for side in (0, 1):
            copy(side, j).start()
    for j in (2, 1, 3, 0):
        for side in (0, 1):
            copy(side, j).wait()
        value = jnp.dot(
            hidden[:, :512], weights[j, 0], preferred_element_type=jnp.float32
        ) + jnp.dot(hidden[:, 512:], weights[j, 1], preferred_element_type=jnp.float32)
        outs[j][...] = value.astype(outs[j].dtype)


def branch(place, hidden, own, other):
    narrow = jax.ShapeDtypeStruct((256, PART), jnp.bfloat16)
    return pl.pallas_call(
        branch_kernel,
        in_specs=[
            pl.BlockSpec(memory_space=pltpu.SMEM),
            pl.BlockSpec(memory_space=pltpu.VMEM),
            pl.BlockSpec(memory_space=pl.ANY),
            pl.BlockSpec(memory_space=pl.ANY),
        ],
        out_specs=[pl.BlockSpec(memory_space=pltpu.VMEM)] * 4,
        out_shape=[jax.ShapeDtypeStruct((256, PART), jnp.float32), narrow, narrow, narrow],
        scratch_shapes=[
            pltpu.VMEM((4, 2, 512, PART), jnp.bfloat16),
            pltpu.SemaphoreType.DMA((4, 2)),
        ],
        compiler_params=pltpu.CompilerParams(vmem_limit_bytes=16 * MIB),
        cost_estimate=pl.CostEstimate(
            flops=2 * 256 * D * 1024, bytes_accessed=5 * MIB, transcendentals=0
        ),
    )(place, hidden, own, other)


def shards(
    teacher_tokens,
    view_index,
    aug_embed,
    norm_gain,
    layer_scale,
    gate_weight,
    up_weight,
    down_weight,
    student_tokens,
    head_weight,
    owner,
):
    group, row, zl = lax.axis_index("group"), lax.axis_index("row"), lax.axis_index("zl")
    images = teacher_tokens.shape[0]
    place = jnp.stack([row, group]).astype(jnp.int32)

    def select(block):
        other = lax.ppermute(block, ("group", "zl"), [(0, 1), (3, 2)])
        return jnp.where(group == zl, block, other)

    def fetch(mine):
        spread = jnp.broadcast_to(mine[None], (16,) + mine.shape)
        return lax.all_to_all(spread, YX, 0, 0, tiled=True).reshape(-1, mine.shape[-1])

    gate_up = select(jnp.concatenate([gate_weight, up_weight], axis=1))
    down = select(down_weight)
    gate_up_own = fetch(gate_up)
    gate_up_other = shift(gate_up_own, "group", 2, 1)
    down, gate_up_own = lax.optimization_barrier((down, gate_up_own))
    down_own = fetch(down)
    down_other = shift(down_own, "group", 2, 1)

    kinds = aug_embed.shape[0]
    kind_table = (
        view_index.reshape(-1)[:, None] == jnp.arange(kinds, dtype=jnp.int32)[None, :]
    ).astype(jnp.bfloat16)
    embedded = jnp.dot(kind_table, aug_embed, preferred_element_type=jnp.float32).reshape(
        images, 4, 1, PART
    )
    shifted = (teacher_tokens.astype(jnp.float32) + embedded).astype(jnp.bfloat16)
    residual = jnp.mean(shifted.astype(jnp.float32), axis=1).reshape(256, PART)
    student = [student_tokens[:, PART * c : PART * c + PART] for c in range(4)]
    own = jnp.concatenate(
        [
            shifted.reshape(2, 512, PART),
            jnp.stack([jnp.concatenate(student[:2]), jnp.concatenate(student[2:])]),
        ],
        axis=1,
    )
    before = shift(own, "row", 4, 1)
    after = shift(own, "row", 4, -1)
    far_top = shift(before[0], "row", 4, 1)
    far_bottom = shift(after[1], "row", 4, -1)

    gain = norm_gain.astype(jnp.float32).reshape(1, D)
    normed = norm(place, own, after, before, far_top, far_bottom, gain)
    hidden = hidden_mean(place, normed, gate_up_own, gate_up_other)
    part, *away = branch(place, hidden, down_own, down_other)
    got = [shift(away[j - 1], "row", 4, j) for j in (2, 1, 3)]

    def pupil(halves):
        return jnp.stack(
            [jnp.concatenate([half[512:544], half[544:576]], axis=1) for half in halves]
        )

    pupils = [pupil(own), pupil(after), pupil((far_top, far_bottom)), pupil(before)]
    pupils = jnp.stack(pupils + pupils)
    pupils = lax.dynamic_slice_in_dim(pupils, 4 - row, 4, axis=0)
    pupils = pupils.reshape(8, images, SW).transpose(1, 0, 2).reshape(256, SW)
    head = jnp.dot(pupils, head_weight, preferred_element_type=jnp.float32)

    averaged = part + sum(piece.astype(jnp.float32) for piece in got)
    target = (residual + layer_scale.astype(jnp.float32) * averaged).astype(jnp.bfloat16)
    target = target.astype(jnp.float32)
    sums = jnp.stack(
        [
            jnp.sum(head, axis=1),
            jnp.sum(head * head, axis=1),
            jnp.sum(target, axis=1),
            jnp.sum(head * target, axis=1),
            jnp.sum(target * target, axis=1),
        ]
    )
    sums = jnp.sum(lax.all_gather(sums, "row"), axis=0)
    center = sums[0] / D
    spread = sums[1] / D - center * center
    scaler = lax.rsqrt(spread + 1e-05)
    pred_square = scaler * scaler * (sums[1] - D * center * center)
    pred_target = scaler * (sums[3] - center * sums[2])
    diff_square = pred_square - 2.0 * pred_target + sums[4]
    mean_first = -2.0 / IMAGES * sums[2] / D
    mean_second = 2.0 / IMAGES * (pred_square - pred_target) / D
    pred = (head - center[:, None]) * scaler[:, None]
    dpred = 2.0 / IMAGES * (pred - target)
    dz = (
        scaler[:, None] * (dpred - mean_first[:, None] - pred * mean_second[:, None])
    ).astype(jnp.bfloat16)
    errors = jnp.sum(diff_square.reshape(images, 8), axis=1) / (8 * D)
    mine = owner == jnp.arange(32, dtype=jnp.int32)[None, :]
    loss = jnp.sum(jnp.where(mine, errors[:, None], 0.0), axis=0)
    loss_high = loss.astype(jnp.bfloat16)
    loss_low = (loss - loss_high.astype(jnp.float32)).astype(jnp.bfloat16)

    grad = lax.dot_general(pupils, dz, (((0,), (0,)), ((), ())), preferred_element_type=jnp.float32)
    grad = grad.reshape(2, PART, PART)
    keep = lax.dynamic_index_in_dim(grad, group, 0, keepdims=False)
    give = lax.dynamic_index_in_dim(grad, 1 - group, 0, keepdims=False)
    half = keep + shift(give.astype(jnp.bfloat16), "group", 2, 1).astype(jnp.float32)
    half = half.astype(jnp.bfloat16).reshape(32, 12, PART)
    note = jnp.stack([loss_high, loss_low], axis=1)[:, :, None]
    note = jnp.broadcast_to(note, (32, 2, PART))
    packet = jnp.concatenate([half, note], axis=1)
    packet = lax.all_to_all(packet, COL, 0, 0, tiled=True).astype(jnp.float32)
    summed = jnp.sum(packet, axis=0)
    owner_loss = summed[12, :1] + summed[13, :1]
    piece = summed[:12].astype(jnp.bfloat16)
    piece = lax.all_to_all(jnp.broadcast_to(piece[None], (32, 12, PART)), COL, 0, 0, tiled=True)
    piece = piece.reshape(PART, PART)
    twin = shift(piece, "group", 2, 1)
    head_grad = jnp.concatenate(
        [jnp.where(group == 0, piece, twin), jnp.where(group == 0, twin, piece)], axis=0
    ).astype(jnp.float32)
    return (head_grad, owner_loss)


def solution(mesh):
    fine = Mesh(mesh.devices.reshape(2, 4, 2, 4, 4), ("group", "row", "zl", "y", "x"))
    return jax.shard_map(
        shards,
        mesh=fine,
        in_specs=(
            P(EVERY, None, None, "row"),
            P(EVERY, None),
            P(None, "row"),
            P(),
            P("row"),
            P(COL, "row"),
            P(COL, "row"),
            P(("row",) + COL, None),
            P(EVERY, "row"),
            P(None, "row"),
            P(EVERY, None),
        ),
        out_specs=(P(None, "row"), P(EVERY)),
        check_vma=False,
    )
```

```python
import jax
import jax.numpy as jnp
from jax import lax
from jax.experimental import pallas as pl
from jax.experimental.pallas import tpu as pltpu
from jax.sharding import Mesh, PartitionSpec as P

D = 1536
SW = 768
PART = 384
YX = ("y", "x")
COL = ("zl", "y", "x")
EVERY = ("group", "zl", "y", "x")
IMAGES = 2048
MIB = 1024 * 1024


def shift(value, axis, size, by):
    return lax.ppermute(value, axis, [(i, (i + by) % size) for i in range(size)])


def norm_kernel(place, own, after, before, far_top, far_bottom, gain, out):
    row, group = place[0], place[1]
    far = jnp.where(pl.program_id(0) < 2, far_top[...], far_bottom[...])
    pieces = [own[0], after[0], far, before[0]]
    pieces = [piece.astype(jnp.float32) for piece in pieces]
    total = sum(jnp.sum(piece, axis=1, keepdims=True) for piece in pieces)
    mean = total * (1.0 / D)
    pieces = [piece - mean for piece in pieces]
    square = sum(jnp.sum(piece * piece, axis=1, keepdims=True) for piece in pieces)
    scale = lax.rsqrt(square * (1.0 / D) + 1e-06)
    for j, piece in enumerate(pieces):
        block = lax.rem(row + j, 4)
        source = pl.multiple_of(block * PART, PART)
        target = pl.multiple_of(lax.rem(block + 2 * group, 4) * PART, PART)
        value = piece * scale * gain[:, pl.ds(source, PART)]
        out[:, pl.ds(target, PART)] = value.astype(jnp.bfloat16)


def norm(place, own, after, before, far_top, far_bottom, gain):
    piece = pl.BlockSpec((1, 256, PART), lambda b: (b // 2, b % 2, 0))
    return pl.pallas_call(
        norm_kernel,
        grid=(4,),
        in_specs=[
            pl.BlockSpec(memory_space=pltpu.SMEM),
            piece,
            piece,
            piece,
            pl.BlockSpec((256, PART), lambda b: (jnp.minimum(b, 1), 0)),
            pl.BlockSpec((256, PART), lambda b: (jnp.maximum(b - 2, 0), 0)),
            pl.BlockSpec((1, D), lambda b: (0, 0)),
        ],
        out_specs=pl.BlockSpec((256, D), lambda b: (b, 0)),
        out_shape=jax.ShapeDtypeStruct((1024, D), jnp.bfloat16),
        compiler_params=pltpu.CompilerParams(vmem_limit_bytes=24 * MIB),
        cost_estimate=pl.CostEstimate(
            flops=30 * 10**9, bytes_accessed=4 * 1024 * D, transcendentals=0
        ),
    )(place, own, after, before, far_top, far_bottom, gain)


SPANS = ((0, 512), (1024, 512), (512, 512), (1536, 512), (2048, 1024))


def branch_kernel(place, normed, *refs):
    row, group, y, x = place[0], place[1], place[2], place[3]
    sources = (refs[:4], refs[4:8])
    part, away1, away2, away3 = refs[8:12]
    weights, hidden, down, sems = refs[12:]

    def copy(side, k, span, along_y):
        start, width = SPANS[span]
        columns = pl.ds(start, width)
        block = weights.at[side]
        if along_y:
            block = block.at[lax.rem(y + k, 4), :, :, columns]
        else:
            block = block.at[:, lax.rem(x + k, 4), :, columns]
        return pltpu.make_async_copy(
            sources[side][k].at[:, :, columns], block, sems.at[side, k, span]
        )

    def start_all(side, along_y, span):
        for k in range(4):
            copy(side, k, span, along_y).start()

    def wait_all(spans):
        for span in spans:
            for side in (0, 1):
                for k in range(4):
                    copy(side, k, span, True).wait()

    for span in range(5):
        for side in (0, 1):
            along = group == side

            @pl.when(along)
            def _():
                start_all(side, True, span)

            @pl.when(jnp.logical_not(along))
            def _():
                start_all(side, False, span)

    def project(kind, n):
        start = kind * 1024 + n * 256
        return sum(
            jnp.dot(
                normed[:, 768 * side : 768 * side + 768],
                weights[side, :, :, :, start : start + 256].reshape(768, 256),
                preferred_element_type=jnp.float32,
            )
            for side in (0, 1)
        )

    for n in range(4):
        if n == 0:
            wait_all((0, 1))
        if n == 2:
            wait_all((2, 3))
        gate = project(0, n)
        upward = project(1, n)
        value = gate * upward / (1.0 + jnp.exp(-gate))
        value = jnp.sum(value.reshape(32, 4, 8, 256), axis=1).reshape(256, 256) * 0.25
        target = pl.multiple_of(lax.rem(n + 2 * group, 4) * 256, 256)
        hidden[:, pl.ds(target, 256)] = value.astype(jnp.bfloat16)

    wait_all((4,))

    def unpack(c, carry):
        rows = pl.multiple_of(c * 32, 32)
        for side in (0, 1):
            half = weights.at[side, c // 4, lax.rem(c, 4)]
            down[pl.ds(side * 512 + rows, 32), 0:1024] = half[0:32, 2048:3072]
            tail = half[32:48, 2048:3072]
            down[pl.ds(side * 512 + rows, 16), 1024:1536] = tail[:, :512]
            down[pl.ds(side * 512 + rows + 16, 16), 1024:1536] = tail[:, 512:]
        return carry

    lax.fori_loop(0, 16, unpack, 0)
    for j, out in ((2, away2), (1, away1), (3, away3), (0, part)):
        start = pl.multiple_of(lax.rem(row + j, 4) * PART, PART)
        value = jnp.dot(
            hidden[...], down[:, pl.ds(start, PART)], preferred_element_type=jnp.float32
        )
        out[...] = value.astype(out.dtype)


def branch(place, normed, own, other):
    narrow = jax.ShapeDtypeStruct((256, PART), jnp.bfloat16)
    vmem = pl.BlockSpec(memory_space=pltpu.VMEM)
    return pl.pallas_call(
        branch_kernel,
        in_specs=[pl.BlockSpec(memory_space=pltpu.SMEM), vmem]
        + [pl.BlockSpec(memory_space=pl.ANY)] * 8,
        out_specs=[vmem] * 4,
        out_shape=[jax.ShapeDtypeStruct((256, PART), jnp.float32), narrow, narrow, narrow],
        scratch_shapes=[
            pltpu.VMEM((2, 4, 4, 48, 3072), jnp.bfloat16),
            pltpu.VMEM((256, 1024), jnp.bfloat16),
            pltpu.VMEM((1024, D), jnp.bfloat16),
            pltpu.SemaphoreType.DMA((2, 4, 5)),
        ],
        compiler_params=pltpu.CompilerParams(vmem_limit_bytes=40 * MIB),
        cost_estimate=pl.CostEstimate(
            flops=2 * 1024 * D * 2048, bytes_accessed=10 * MIB, transcendentals=1024 * 1024
        ),
    )(place, normed, *own, *other)


def gather_kernel(place, *refs):
    sources, out = refs[:4], refs[4]
    position = jnp.where(place[1] == 0, place[3], place[2])
    for k, source in enumerate(sources):
        out[lax.rem(position + k, 4)] = source[...]


def gather(place, blocks):
    vmem = pl.BlockSpec(memory_space=pltpu.VMEM)
    return pl.pallas_call(
        gather_kernel,
        in_specs=[pl.BlockSpec(memory_space=pltpu.SMEM)] + [vmem] * 4,
        out_specs=vmem,
        out_shape=jax.ShapeDtypeStruct((4,) + blocks[0].shape, jnp.bfloat16),
        compiler_params=pltpu.CompilerParams(vmem_limit_bytes=16 * MIB),
        cost_estimate=pl.CostEstimate(flops=0, bytes_accessed=3 * MIB, transcendentals=0),
    )(place, *blocks)


def student_kernel(place, own, after, before, far_top, far_bottom, weight, pupils, head, gathered):
    row = place[0]
    pieces = (
        (own[0], own[1]),
        (after[0], after[1]),
        (far_top[...], far_bottom[...]),
        (before[0], before[1]),
    )
    for j, piece in enumerate(pieces):
        for i, half in enumerate(piece):
            rows = (2 * j + i) * 32
            gathered[rows : rows + 32, 0:PART] = half[0:32]
            gathered[rows : rows + 32, PART:SW] = half[32:64]
    target = lax.broadcasted_iota(jnp.int32, (256, 256), 0)
    source = lax.broadcasted_iota(jnp.int32, (256, 256), 1)
    image, patch = target // 8, lax.rem(target, 8)
    place_of = lax.rem(patch - 2 * row + 8, 8) * 32 + image
    order = jnp.where(source == place_of, 1.0, 0.0).astype(jnp.bfloat16)
    value = jnp.dot(order, gathered[...], preferred_element_type=jnp.float32)
    value = value.astype(jnp.bfloat16)
    pupils[...] = value
    head[...] = jnp.dot(value, weight[...], preferred_element_type=jnp.float32)


def student(place, own, after, before, far_top, far_bottom, weight):
    piece = pl.BlockSpec((2, 64, PART), lambda b: (0, 8, 0))
    half = pl.BlockSpec((64, PART), lambda b: (8, 0))
    return pl.pallas_call(
        student_kernel,
        grid=(1,),
        in_specs=[
            pl.BlockSpec(memory_space=pltpu.SMEM),
            piece,
            piece,
            piece,
            half,
            half,
            pl.BlockSpec((SW, PART), lambda b: (0, 0)),
        ],
        out_specs=[
            pl.BlockSpec((256, SW), lambda b: (0, 0)),
            pl.BlockSpec((256, PART), lambda b: (0, 0)),
        ],
        out_shape=[
            jax.ShapeDtypeStruct((256, SW), jnp.bfloat16),
            jax.ShapeDtypeStruct((256, PART), jnp.float32),
        ],
        scratch_shapes=[pltpu.VMEM((256, SW), jnp.bfloat16)],
        compiler_params=pltpu.CompilerParams(vmem_limit_bytes=16 * MIB),
        cost_estimate=pl.CostEstimate(
            flops=2 * 256 * SW * 640, bytes_accessed=2 * MIB, transcendentals=0
        ),
    )(place, own, after, before, far_top, far_bottom, weight)


def shards(
    teacher_tokens,
    view_index,
    aug_embed,
    norm_gain,
    layer_scale,
    gate_weight,
    up_weight,
    down_weight,
    student_tokens,
    head_weight,
    owner,
):
    group, row, zl = lax.axis_index("group"), lax.axis_index("row"), lax.axis_index("zl")
    images = teacher_tokens.shape[0]
    place = jnp.stack([row, group, lax.axis_index("y"), lax.axis_index("x")]).astype(jnp.int32)

    down = jnp.concatenate(
        [
            down_weight[:, :1024],
            jnp.concatenate([down_weight[:16, 1024:], down_weight[16:, 1024:]], axis=1),
        ],
        axis=0,
    )
    block = jnp.concatenate([gate_weight, up_weight, down], axis=1)
    twin = lax.ppermute(block, ("group", "zl"), [(0, 1), (3, 2)])
    block = jnp.where(group == zl, block, twin)
    def collect(value, first):
        pieces = [value]
        for by in (-1, 2, 1):
            pairs = []
            for y in range(4):
                for x in range(4):
                    along_x = (y, (x + by) % 4)
                    along_y = ((y + by) % 4, x)
                    for core, (to_y, to_x) in enumerate(
                        (along_x, along_y) if first else (along_y, along_x)
                    ):
                        pairs.append((core * 16 + y * 4 + x, core * 16 + to_y * 4 + to_x))
            pieces.append(lax.ppermute(value, ("group", "y", "x"), pairs))
        return pieces

    weights_own = collect(gather(place, collect(block, True)), False)
    weights_other = [shift(piece, "group", 2, 1) for piece in weights_own]

    kinds = aug_embed.shape[0]
    kind_table = (
        view_index.reshape(-1)[:, None] == jnp.arange(kinds, dtype=jnp.int32)[None, :]
    ).astype(jnp.bfloat16)
    embedded = jnp.dot(kind_table, aug_embed, preferred_element_type=jnp.float32).reshape(
        images, 4, 1, PART
    )
    shifted = (teacher_tokens.astype(jnp.float32) + embedded).astype(jnp.bfloat16)
    residual = jnp.mean(shifted.astype(jnp.float32), axis=1).reshape(256, PART)
    quarters = [student_tokens[:, PART * c : PART * c + PART] for c in range(4)]
    own = jnp.concatenate(
        [
            shifted.reshape(2, 512, PART),
            jnp.stack([jnp.concatenate(quarters[:2]), jnp.concatenate(quarters[2:])]),
        ],
        axis=1,
    )
    own, twin = lax.optimization_barrier((own, twin))
    before = shift(own, "row", 4, 1)
    after = shift(own, "row", 4, -1)
    far_top = shift(before[0], "row", 4, 1)
    far_bottom = shift(after[1], "row", 4, -1)

    gain = norm_gain.astype(jnp.float32).reshape(1, D)
    normed = norm(place, own, after, before, far_top, far_bottom, gain)
    part, *away = branch(place, normed, weights_own, weights_other)
    held = (own, after, before, far_top, far_bottom)
    away, held = lax.optimization_barrier((away, held))
    got = [shift(away[j - 1], "row", 4, j) for j in (2, 1, 3)]
    pupils, head = student(place, *held, head_weight)

    averaged = part + sum(piece.astype(jnp.float32) for piece in got)
    target = (residual + layer_scale.astype(jnp.float32) * averaged).astype(jnp.bfloat16)
    target = target.astype(jnp.float32)
    sums = jnp.stack(
        [
            jnp.sum(head, axis=1),
            jnp.sum(head * head, axis=1),
            jnp.sum(target, axis=1),
            jnp.sum(head * target, axis=1),
            jnp.sum(target * target, axis=1),
        ]
    )
    sums = jnp.sum(lax.all_gather(sums, "row"), axis=0)
    center = sums[0] / D
    spread = sums[1] / D - center * center
    scaler = lax.rsqrt(spread + 1e-05)
    pred_square = scaler * scaler * (sums[1] - D * center * center)
    pred_target = scaler * (sums[3] - center * sums[2])
    diff_square = pred_square - 2.0 * pred_target + sums[4]
    mean_first = -2.0 / IMAGES * sums[2] / D
    mean_second = 2.0 / IMAGES * (pred_square - pred_target) / D
    pred = (head - center[:, None]) * scaler[:, None]
    dpred = 2.0 / IMAGES * (pred - target)
    dz = (
        scaler[:, None] * (dpred - mean_first[:, None] - pred * mean_second[:, None])
    ).astype(jnp.bfloat16)
    errors = jnp.sum(diff_square.reshape(images, 8), axis=1) / (8 * D)
    mine = owner == jnp.arange(32, dtype=jnp.int32)[None, :]
    loss = jnp.sum(jnp.where(mine, errors[:, None], 0.0), axis=0)
    loss_high = loss.astype(jnp.bfloat16)
    loss_low = (loss - loss_high.astype(jnp.float32)).astype(jnp.bfloat16)

    grad = lax.dot_general(pupils, dz, (((0,), (0,)), ((), ())), preferred_element_type=jnp.float32)
    grad = grad.reshape(2, PART, PART)
    keep = lax.dynamic_index_in_dim(grad, group, 0, keepdims=False)
    give = lax.dynamic_index_in_dim(grad, 1 - group, 0, keepdims=False)
    half = keep + shift(give.astype(jnp.bfloat16), "group", 2, 1).astype(jnp.float32)
    half = half.astype(jnp.bfloat16).reshape(32, 12, PART)
    note = jnp.stack([loss_high, loss_low], axis=1)[:, :, None]
    note = jnp.broadcast_to(note, (32, 2, PART))
    packet = jnp.concatenate([half, note], axis=1)
    packet = lax.all_to_all(packet, COL, 0, 0, tiled=True).astype(jnp.float32)
    summed = jnp.sum(packet, axis=0)
    owner_loss = summed[12, :1] + summed[13, :1]
    piece = summed[:12].astype(jnp.bfloat16)
    piece = lax.all_to_all(jnp.broadcast_to(piece[None], (32, 12, PART)), COL, 0, 0, tiled=True)
    piece = piece.reshape(PART, PART)
    other = shift(piece, "group", 2, 1)
    head_grad = jnp.concatenate(
        [jnp.where(group == 0, piece, other), jnp.where(group == 0, other, piece)], axis=0
    ).astype(jnp.float32)
    return (head_grad, owner_loss)


def solution(mesh):
    fine = Mesh(mesh.devices.reshape(2, 4, 2, 4, 4), ("group", "row", "zl", "y", "x"))
    return jax.shard_map(
        shards,
        mesh=fine,
        in_specs=(
            P(EVERY, None, None, "row"),
            P(EVERY, None),
            P(None, "row"),
            P(),
            P("row"),
            P(COL, "row"),
            P(COL, "row"),
            P(("row",) + COL, None),
            P(EVERY, "row"),
            P(None, "row"),
            P(EVERY, None),
        ),
        out_specs=(P(None, "row"), P(EVERY)),
        check_vma=False,
    )
```

```python
import jax
import jax.numpy as jnp
from jax import lax
from jax.experimental import pallas as pl
from jax.experimental.pallas import tpu as pltpu
from jax.sharding import Mesh, PartitionSpec as P

D = 1536
SW = 768
PART = 384
YX = ("y", "x")
COL = ("zl", "y", "x")
EVERY = ("group", "zl", "y", "x")
IMAGES = 2048
MIB = 1024 * 1024


def shift(value, axis, size, by):
    return lax.ppermute(value, axis, [(i, (i + by) % size) for i in range(size)])


def norm_kernel(place, own, after, before, far_top, far_bottom, gain, out):
    row, group = place[0], place[1]
    far = jnp.where(pl.program_id(0) < 2, far_top[...], far_bottom[...])
    pieces = [own[0], after[0], far, before[0]]
    pieces = [piece.astype(jnp.float32) for piece in pieces]
    total = sum(jnp.sum(piece, axis=1, keepdims=True) for piece in pieces)
    mean = total * (1.0 / D)
    pieces = [piece - mean for piece in pieces]
    square = sum(jnp.sum(piece * piece, axis=1, keepdims=True) for piece in pieces)
    scale = lax.rsqrt(square * (1.0 / D) + 1e-06)
    for j, piece in enumerate(pieces):
        block = lax.rem(row + j, 4)
        source = pl.multiple_of(block * PART, PART)
        target = pl.multiple_of(lax.rem(block + 2 * group, 4) * PART, PART)
        value = piece * scale * gain[:, pl.ds(source, PART)]
        out[:, pl.ds(target, PART)] = value.astype(jnp.bfloat16)


def norm(place, own, after, before, far_top, far_bottom, gain):
    piece = pl.BlockSpec((1, 256, PART), lambda b: (b // 2, b % 2, 0))
    return pl.pallas_call(
        norm_kernel,
        grid=(4,),
        in_specs=[
            pl.BlockSpec(memory_space=pltpu.SMEM),
            piece,
            piece,
            piece,
            pl.BlockSpec((256, PART), lambda b: (jnp.minimum(b, 1), 0)),
            pl.BlockSpec((256, PART), lambda b: (jnp.maximum(b - 2, 0), 0)),
            pl.BlockSpec((1, D), lambda b: (0, 0)),
        ],
        out_specs=pl.BlockSpec((256, D), lambda b: (b, 0)),
        out_shape=jax.ShapeDtypeStruct((1024, D), jnp.bfloat16),
        compiler_params=pltpu.CompilerParams(vmem_limit_bytes=24 * MIB),
        cost_estimate=pl.CostEstimate(
            flops=30 * 10**9, bytes_accessed=4 * 1024 * D, transcendentals=0
        ),
    )(place, own, after, before, far_top, far_bottom, gain)


SPANS = ((0, 512), (1024, 512), (512, 512), (1536, 512), (2048, 1024))


def branch_kernel(place, normed, *refs):
    row, group, y, x = place[0], place[1], place[2], place[3]
    sources = (refs[:4], refs[4:8])
    part, away1, away2, away3 = refs[8:12]
    weights, hidden, down, sems = refs[12:]

    def copy(side, k, span, along_y):
        start, width = SPANS[span]
        columns = pl.ds(start, width)
        block = weights.at[side]
        if along_y:
            block = block.at[lax.rem(y + k, 4), :, :, columns]
        else:
            block = block.at[:, lax.rem(x + k, 4), :, columns]
        return pltpu.make_async_copy(
            sources[side][k].at[:, :, columns], block, sems.at[side, k, span]
        )

    def start_all(side, along_y, span):
        for k in range(4):
            copy(side, k, span, along_y).start()

    def wait_all(spans):
        for span in spans:
            for side in (0, 1):
                for k in range(4):
                    copy(side, k, span, True).wait()

    for span in range(5):
        for side in (0, 1):
            along = group == side

            @pl.when(along)
            def _():
                start_all(side, True, span)

            @pl.when(jnp.logical_not(along))
            def _():
                start_all(side, False, span)

    def project(kind, n):
        start = kind * 1024 + n * 256
        return sum(
            jnp.dot(
                normed[:, 768 * side : 768 * side + 768],
                weights[side, :, :, :, start : start + 256].reshape(768, 256),
                preferred_element_type=jnp.float32,
            )
            for side in (0, 1)
        )

    for n in range(4):
        if n == 0:
            wait_all((0, 1))
        if n == 2:
            wait_all((2, 3))
        gate = project(0, n)
        upward = project(1, n)
        value = gate * upward / (1.0 + jnp.exp(-gate))
        value = jnp.sum(value.reshape(32, 4, 8, 256), axis=1).reshape(256, 256) * 0.25
        target = pl.multiple_of(lax.rem(n + 2 * group, 4) * 256, 256)
        hidden[:, pl.ds(target, 256)] = value.astype(jnp.bfloat16)

    wait_all((4,))

    def unpack(c, carry):
        rows = pl.multiple_of(c * 32, 32)
        for side in (0, 1):
            half = weights.at[side, c // 4, lax.rem(c, 4)]
            down[pl.ds(side * 512 + rows, 32), 0:1024] = half[0:32, 2048:3072]
            tail = half[32:48, 2048:3072]
            down[pl.ds(side * 512 + rows, 16), 1024:1536] = tail[:, :512]
            down[pl.ds(side * 512 + rows + 16, 16), 1024:1536] = tail[:, 512:]
        return carry

    lax.fori_loop(0, 16, unpack, 0)
    for j, out in ((2, away2), (1, away1), (3, away3), (0, part)):
        start = pl.multiple_of(lax.rem(row + j, 4) * PART, PART)
        value = jnp.dot(
            hidden[...], down[:, pl.ds(start, PART)], preferred_element_type=jnp.float32
        )
        out[...] = value.astype(out.dtype)


def branch(place, normed, own, other):
    narrow = jax.ShapeDtypeStruct((256, PART), jnp.bfloat16)
    vmem = pl.BlockSpec(memory_space=pltpu.VMEM)
    return pl.pallas_call(
        branch_kernel,
        in_specs=[pl.BlockSpec(memory_space=pltpu.SMEM), vmem]
        + [pl.BlockSpec(memory_space=pl.ANY)] * 8,
        out_specs=[vmem] * 4,
        out_shape=[jax.ShapeDtypeStruct((256, PART), jnp.float32), narrow, narrow, narrow],
        scratch_shapes=[
            pltpu.VMEM((2, 4, 4, 48, 3072), jnp.bfloat16),
            pltpu.VMEM((256, 1024), jnp.bfloat16),
            pltpu.VMEM((1024, D), jnp.bfloat16),
            pltpu.SemaphoreType.DMA((2, 4, 5)),
        ],
        compiler_params=pltpu.CompilerParams(vmem_limit_bytes=40 * MIB),
        cost_estimate=pl.CostEstimate(
            flops=2 * 1024 * D * 2048, bytes_accessed=10 * MIB, transcendentals=1024 * 1024
        ),
    )(place, normed, *own, *other)


def gather_kernel(place, *refs):
    sources, out = refs[:4], refs[4]
    position = jnp.where(place[1] == 0, place[3], place[2])
    for k, source in enumerate(sources):
        out[lax.rem(position + k, 4)] = source[...]


def gather(place, blocks):
    vmem = pl.BlockSpec(memory_space=pltpu.VMEM)
    return pl.pallas_call(
        gather_kernel,
        in_specs=[pl.BlockSpec(memory_space=pltpu.SMEM)] + [vmem] * 4,
        out_specs=vmem,
        out_shape=jax.ShapeDtypeStruct((4,) + blocks[0].shape, jnp.bfloat16),
        compiler_params=pltpu.CompilerParams(vmem_limit_bytes=16 * MIB),
        cost_estimate=pl.CostEstimate(flops=0, bytes_accessed=3 * MIB, transcendentals=0),
    )(place, *blocks)


def student_kernel(place, own, after, before, far_top, far_bottom, weight, pupils, head, gathered):
    row = place[0]
    pieces = (
        (own[0], own[1]),
        (after[0], after[1]),
        (far_top[...], far_bottom[...]),
        (before[0], before[1]),
    )
    for j, piece in enumerate(pieces):
        for i, half in enumerate(piece):
            rows = (2 * j + i) * 32
            gathered[rows : rows + 32, 0:PART] = half[0:32]
            gathered[rows : rows + 32, PART:SW] = half[32:64]
    target = lax.broadcasted_iota(jnp.int32, (256, 256), 0)
    source = lax.broadcasted_iota(jnp.int32, (256, 256), 1)
    image, patch = target // 8, lax.rem(target, 8)
    place_of = lax.rem(patch - 2 * row + 8, 8) * 32 + image
    order = jnp.where(source == place_of, 1.0, 0.0).astype(jnp.bfloat16)
    value = jnp.dot(order, gathered[...], preferred_element_type=jnp.float32)
    value = value.astype(jnp.bfloat16)
    pupils[...] = value
    head[...] = jnp.dot(value, weight[...], preferred_element_type=jnp.float32)


def student(place, own, after, before, far_top, far_bottom, weight):
    piece = pl.BlockSpec((2, 64, PART), lambda b: (0, 8, 0))
    half = pl.BlockSpec((64, PART), lambda b: (8, 0))
    return pl.pallas_call(
        student_kernel,
        grid=(1,),
        in_specs=[
            pl.BlockSpec(memory_space=pltpu.SMEM),
            piece,
            piece,
            piece,
            half,
            half,
            pl.BlockSpec((SW, PART), lambda b: (0, 0)),
        ],
        out_specs=[
            pl.BlockSpec((256, SW), lambda b: (0, 0)),
            pl.BlockSpec((256, PART), lambda b: (0, 0)),
        ],
        out_shape=[
            jax.ShapeDtypeStruct((256, SW), jnp.bfloat16),
            jax.ShapeDtypeStruct((256, PART), jnp.float32),
        ],
        scratch_shapes=[pltpu.VMEM((256, SW), jnp.bfloat16)],
        compiler_params=pltpu.CompilerParams(vmem_limit_bytes=16 * MIB),
        cost_estimate=pl.CostEstimate(
            flops=2 * 256 * SW * 640, bytes_accessed=2 * MIB, transcendentals=0
        ),
    )(place, own, after, before, far_top, far_bottom, weight)


def shards(
    teacher_tokens,
    view_index,
    aug_embed,
    norm_gain,
    layer_scale,
    gate_weight,
    up_weight,
    down_weight,
    student_tokens,
    head_weight,
    owner,
):
    group, row, zl = lax.axis_index("group"), lax.axis_index("row"), lax.axis_index("zl")
    images = teacher_tokens.shape[0]
    place = jnp.stack([row, group, lax.axis_index("y"), lax.axis_index("x")]).astype(jnp.int32)

    down = jnp.concatenate(
        [
            down_weight[:, :1024],
            jnp.concatenate([down_weight[:16, 1024:], down_weight[16:, 1024:]], axis=1),
        ],
        axis=0,
    )
    block = jnp.concatenate([gate_weight, up_weight, down], axis=1)
    twin = lax.ppermute(block, ("group", "zl"), [(0, 1), (3, 2)])
    block = jnp.where(group == zl, block, twin)
    def collect(value, first):
        pieces = [value]
        for by in (-1, 2, 1):
            pairs = []
            for y in range(4):
                for x in range(4):
                    along_x = (y, (x + by) % 4)
                    along_y = ((y + by) % 4, x)
                    for core, (to_y, to_x) in enumerate(
                        (along_x, along_y) if first else (along_y, along_x)
                    ):
                        pairs.append((core * 16 + y * 4 + x, core * 16 + to_y * 4 + to_x))
            pieces.append(lax.ppermute(value, ("group", "y", "x"), pairs))
        return pieces

    line = gather(place, collect(block, True))
    weights_own = collect(line, False)
    both = lax.all_to_all(
        jnp.broadcast_to(line[None], (2,) + line.shape), "group", 0, 0, tiled=True
    )
    weights_other = [lax.dynamic_index_in_dim(both, 1 - group, 0, keepdims=False)]
    weights_other += [shift(piece, "group", 2, 1) for piece in weights_own[1:]]

    kinds = aug_embed.shape[0]
    kind_table = (
        view_index.reshape(-1)[:, None] == jnp.arange(kinds, dtype=jnp.int32)[None, :]
    ).astype(jnp.bfloat16)
    embedded = jnp.dot(kind_table, aug_embed, preferred_element_type=jnp.float32).reshape(
        images, 4, 1, PART
    )
    shifted = (teacher_tokens.astype(jnp.float32) + embedded).astype(jnp.bfloat16)
    residual = jnp.mean(shifted.astype(jnp.float32), axis=1).reshape(256, PART)
    quarters = [student_tokens[:, PART * c : PART * c + PART] for c in range(4)]
    own = jnp.concatenate(
        [
            shifted.reshape(2, 512, PART),
            jnp.stack([jnp.concatenate(quarters[:2]), jnp.concatenate(quarters[2:])]),
        ],
        axis=1,
    )
    own, twin = lax.optimization_barrier((own, twin))
    before = shift(own, "row", 4, 1)
    after = shift(own, "row", 4, -1)
    far_top = shift(before[0], "row", 4, 1)
    far_bottom = shift(after[1], "row", 4, -1)

    gain = norm_gain.astype(jnp.float32).reshape(1, D)
    normed = norm(place, own, after, before, far_top, far_bottom, gain)
    part, *away = branch(place, normed, weights_own, weights_other)
    held = (own, after, before, far_top, far_bottom)
    away, held = lax.optimization_barrier((away, held))
    got = [shift(away[j - 1], "row", 4, j) for j in (2, 1, 3)]
    pupils, head = student(place, *held, head_weight)

    averaged = part + sum(piece.astype(jnp.float32) for piece in got)
    target = (residual + layer_scale.astype(jnp.float32) * averaged).astype(jnp.bfloat16)
    target = target.astype(jnp.float32)
    sums = jnp.stack(
        [
            jnp.sum(head, axis=1),
            jnp.sum(head * head, axis=1),
            jnp.sum(target, axis=1),
            jnp.sum(head * target, axis=1),
            jnp.sum(target * target, axis=1),
        ]
    )
    sums = sums + lax.ppermute(sums, "row", [(0, 1), (1, 0), (2, 3), (3, 2)])
    sums = sums + lax.ppermute(sums, "row", [(0, 2), (1, 3), (2, 0), (3, 1)])
    center = sums[0] / D
    spread = sums[1] / D - center * center
    scaler = lax.rsqrt(spread + 1e-05)
    pred_square = scaler * scaler * (sums[1] - D * center * center)
    pred_target = scaler * (sums[3] - center * sums[2])
    diff_square = pred_square - 2.0 * pred_target + sums[4]
    mean_first = -2.0 / IMAGES * sums[2] / D
    mean_second = 2.0 / IMAGES * (pred_square - pred_target) / D
    pred = (head - center[:, None]) * scaler[:, None]
    dpred = 2.0 / IMAGES * (pred - target)
    dz = (
        scaler[:, None] * (dpred - mean_first[:, None] - pred * mean_second[:, None])
    ).astype(jnp.bfloat16)
    errors = jnp.sum(diff_square.reshape(images, 8), axis=1) / (8 * D)
    mine = owner == jnp.arange(32, dtype=jnp.int32)[None, :]
    loss = jnp.sum(jnp.where(mine, errors[:, None], 0.0), axis=0)
    loss_high = loss.astype(jnp.bfloat16)
    loss_low = (loss - loss_high.astype(jnp.float32)).astype(jnp.bfloat16)

    grad = lax.dot_general(pupils, dz, (((0,), (0,)), ((), ())), preferred_element_type=jnp.float32)
    grad = grad.reshape(2, PART, PART)
    keep = lax.dynamic_index_in_dim(grad, group, 0, keepdims=False)
    give = lax.dynamic_index_in_dim(grad, 1 - group, 0, keepdims=False)
    half = keep + shift(give.astype(jnp.bfloat16), "group", 2, 1).astype(jnp.float32)
    half = half.astype(jnp.bfloat16).reshape(32, 12, PART)
    note = jnp.stack([loss_high, loss_low], axis=1)[:, :, None]
    note = jnp.broadcast_to(note, (32, 2, PART))
    packet = jnp.concatenate([half, note], axis=1)
    packet = lax.all_to_all(packet, COL, 0, 0, tiled=True).astype(jnp.float32)
    summed = jnp.sum(packet, axis=0)
    owner_loss = summed[12, :1] + summed[13, :1]
    piece = summed[:12].astype(jnp.bfloat16)
    piece = lax.all_to_all(jnp.broadcast_to(piece[None], (32, 12, PART)), COL, 0, 0, tiled=True)
    piece = piece.reshape(PART, PART)
    other = shift(piece, "group", 2, 1)
    head_grad = jnp.concatenate(
        [jnp.where(group == 0, piece, other), jnp.where(group == 0, other, piece)], axis=0
    ).astype(jnp.float32)
    return (head_grad, owner_loss)


def solution(mesh):
    fine = Mesh(mesh.devices.reshape(2, 4, 2, 4, 4), ("group", "row", "zl", "y", "x"))
    return jax.shard_map(
        shards,
        mesh=fine,
        in_specs=(
            P(EVERY, None, None, "row"),
            P(EVERY, None),
            P(None, "row"),
            P(),
            P("row"),
            P(COL, "row"),
            P(COL, "row"),
            P(("row",) + COL, None),
            P(EVERY, "row"),
            P(None, "row"),
            P(EVERY, None),
        ),
        out_specs=(P(None, "row"), P(EVERY)),
        check_vma=False,
    )
```

```python
import jax
import jax.numpy as jnp
from jax import lax
from jax.experimental import pallas as pl
from jax.experimental.pallas import tpu as pltpu
from jax.sharding import Mesh, PartitionSpec as P

D = 1536
SW = 768
PART = 384
YX = ("y", "x")
COL = ("zl", "y", "x")
EVERY = ("group", "zl", "y", "x")
IMAGES = 2048
MIB = 1024 * 1024


def shift(value, axis, size, by):
    return lax.ppermute(value, axis, [(i, (i + by) % size) for i in range(size)])


def norm_kernel(place, own, after, before, far_top, far_bottom, gain, out):
    row, group = place[0], place[1]
    far = jnp.where(pl.program_id(0) < 2, far_top[...], far_bottom[...])
    pieces = [own[0], after[0], far, before[0]]
    pieces = [piece.astype(jnp.float32) for piece in pieces]
    total = sum(jnp.sum(piece, axis=1, keepdims=True) for piece in pieces)
    mean = total * (1.0 / D)
    pieces = [piece - mean for piece in pieces]
    square = sum(jnp.sum(piece * piece, axis=1, keepdims=True) for piece in pieces)
    scale = lax.rsqrt(square * (1.0 / D) + 1e-06)
    for j, piece in enumerate(pieces):
        block = lax.rem(row + j, 4)
        source = pl.multiple_of(block * PART, PART)
        target = pl.multiple_of(lax.rem(block + 2 * group, 4) * PART, PART)
        value = piece * scale * gain[:, pl.ds(source, PART)]
        out[:, pl.ds(target, PART)] = value.astype(jnp.bfloat16)


def norm(place, own, after, before, far_top, far_bottom, gain):
    piece = pl.BlockSpec((1, 256, PART), lambda b: (b // 2, b % 2, 0))
    return pl.pallas_call(
        norm_kernel,
        grid=(4,),
        in_specs=[
            pl.BlockSpec(memory_space=pltpu.SMEM),
            piece,
            piece,
            piece,
            pl.BlockSpec((256, PART), lambda b: (jnp.minimum(b, 1), 0)),
            pl.BlockSpec((256, PART), lambda b: (jnp.maximum(b - 2, 0), 0)),
            pl.BlockSpec((1, D), lambda b: (0, 0)),
        ],
        out_specs=pl.BlockSpec((256, D), lambda b: (b, 0)),
        out_shape=jax.ShapeDtypeStruct((1024, D), jnp.bfloat16),
        compiler_params=pltpu.CompilerParams(vmem_limit_bytes=24 * MIB),
        cost_estimate=pl.CostEstimate(
            flops=30 * 10**9, bytes_accessed=4 * 1024 * D, transcendentals=0
        ),
    )(place, own, after, before, far_top, far_bottom, gain)


SPANS = ((0, 512), (1024, 512), (512, 512), (1536, 512), (2048, 1024))


def branch_kernel(place, normed, *refs):
    row, group, y, x = place[0], place[1], place[2], place[3]
    sources = (refs[:4], refs[4:8])
    part, away1, away2, away3 = refs[8:12]
    weights, hidden, down, sems = refs[12:]

    def copy(side, k, span, along_y):
        start, width = SPANS[span]
        columns = pl.ds(start, width)
        block = weights.at[side]
        if along_y:
            block = block.at[lax.rem(y + k, 4), :, :, columns]
        else:
            block = block.at[:, lax.rem(x + k, 4), :, columns]
        return pltpu.make_async_copy(
            sources[side][k].at[:, :, columns], block, sems.at[side, k, span]
        )

    def start_all(side, along_y, span):
        for k in range(4):
            copy(side, k, span, along_y).start()

    def wait_all(spans):
        for span in spans:
            for side in (0, 1):
                for k in range(4):
                    copy(side, k, span, True).wait()

    for span in range(5):
        for side in (0, 1):
            along = group == side

            @pl.when(along)
            def _():
                start_all(side, True, span)

            @pl.when(jnp.logical_not(along))
            def _():
                start_all(side, False, span)

    def project(kind, n):
        start = kind * 1024 + n * 256
        return sum(
            jnp.dot(
                normed[:, 768 * side : 768 * side + 768],
                weights[side, :, :, :, start : start + 256].reshape(768, 256),
                preferred_element_type=jnp.float32,
            )
            for side in (0, 1)
        )

    for n in range(4):
        if n == 0:
            wait_all((0, 1))
        if n == 2:
            wait_all((2, 3))
        gate = project(0, n)
        upward = project(1, n)
        value = gate * upward / (1.0 + jnp.exp(-gate))
        value = jnp.sum(value.reshape(32, 4, 8, 256), axis=1).reshape(256, 256) * 0.25
        target = pl.multiple_of(lax.rem(n + 2 * group, 4) * 256, 256)
        hidden[:, pl.ds(target, 256)] = value.astype(jnp.bfloat16)

    wait_all((4,))

    def unpack(c, carry):
        rows = pl.multiple_of(c * 32, 32)
        for side in (0, 1):
            half = weights.at[side, c // 4, lax.rem(c, 4)]
            down[pl.ds(side * 512 + rows, 32), 0:1024] = half[0:32, 2048:3072]
            tail = half[32:48, 2048:3072]
            down[pl.ds(side * 512 + rows, 16), 1024:1536] = tail[:, :512]
            down[pl.ds(side * 512 + rows + 16, 16), 1024:1536] = tail[:, 512:]
        return carry

    lax.fori_loop(0, 16, unpack, 0)
    for j, out in ((2, away2), (1, away1), (3, away3), (0, part)):
        start = pl.multiple_of(lax.rem(row + j, 4) * PART, PART)
        value = jnp.dot(
            hidden[...], down[:, pl.ds(start, PART)], preferred_element_type=jnp.float32
        )
        out[...] = value.astype(out.dtype)


def branch(place, normed, own, other):
    narrow = jax.ShapeDtypeStruct((256, PART), jnp.bfloat16)
    vmem = pl.BlockSpec(memory_space=pltpu.VMEM)
    return pl.pallas_call(
        branch_kernel,
        in_specs=[pl.BlockSpec(memory_space=pltpu.SMEM), vmem]
        + [pl.BlockSpec(memory_space=pl.ANY)] * 8,
        out_specs=[vmem] * 4,
        out_shape=[jax.ShapeDtypeStruct((256, PART), jnp.float32), narrow, narrow, narrow],
        scratch_shapes=[
            pltpu.VMEM((2, 4, 4, 48, 3072), jnp.bfloat16),
            pltpu.VMEM((256, 1024), jnp.bfloat16),
            pltpu.VMEM((1024, D), jnp.bfloat16),
            pltpu.SemaphoreType.DMA((2, 4, 5)),
        ],
        compiler_params=pltpu.CompilerParams(vmem_limit_bytes=40 * MIB),
        cost_estimate=pl.CostEstimate(
            flops=2 * 1024 * D * 2048, bytes_accessed=10 * MIB, transcendentals=1024 * 1024
        ),
    )(place, normed, *own, *other)


def gather_kernel(place, *refs):
    sources, out = refs[:4], refs[4]
    position = jnp.where(place[1] == 0, place[3], place[2])
    for k, source in enumerate(sources):
        out[lax.rem(position + k, 4)] = source[...]


def gather(place, blocks):
    vmem = pl.BlockSpec(memory_space=pltpu.VMEM)
    return pl.pallas_call(
        gather_kernel,
        in_specs=[pl.BlockSpec(memory_space=pltpu.SMEM)] + [vmem] * 4,
        out_specs=vmem,
        out_shape=jax.ShapeDtypeStruct((4,) + blocks[0].shape, jnp.bfloat16),
        compiler_params=pltpu.CompilerParams(vmem_limit_bytes=16 * MIB),
        cost_estimate=pl.CostEstimate(flops=0, bytes_accessed=3 * MIB, transcendentals=0),
    )(place, *blocks)


def student_kernel(place, own, after, before, far_top, far_bottom, weight, pupils, head, gathered):
    row = place[0]
    pieces = (
        (own[0], own[1]),
        (after[0], after[1]),
        (far_top[...], far_bottom[...]),
        (before[0], before[1]),
    )
    for j, piece in enumerate(pieces):
        for i, half in enumerate(piece):
            rows = (2 * j + i) * 32
            gathered[rows : rows + 32, 0:PART] = half[0:32]
            gathered[rows : rows + 32, PART:SW] = half[32:64]
    target = lax.broadcasted_iota(jnp.int32, (256, 256), 0)
    source = lax.broadcasted_iota(jnp.int32, (256, 256), 1)
    image, patch = target // 8, lax.rem(target, 8)
    place_of = lax.rem(patch - 2 * row + 8, 8) * 32 + image
    order = jnp.where(source == place_of, 1.0, 0.0).astype(jnp.bfloat16)
    value = jnp.dot(order, gathered[...], preferred_element_type=jnp.float32)
    value = value.astype(jnp.bfloat16)
    pupils[...] = value
    head[...] = jnp.dot(value, weight[...], preferred_element_type=jnp.float32)


def student(place, own, after, before, far_top, far_bottom, weight):
    piece = pl.BlockSpec((2, 64, PART), lambda b: (0, 8, 0))
    half = pl.BlockSpec((64, PART), lambda b: (8, 0))
    return pl.pallas_call(
        student_kernel,
        grid=(1,),
        in_specs=[
            pl.BlockSpec(memory_space=pltpu.SMEM),
            piece,
            piece,
            piece,
            half,
            half,
            pl.BlockSpec((SW, PART), lambda b: (0, 0)),
        ],
        out_specs=[
            pl.BlockSpec((256, SW), lambda b: (0, 0)),
            pl.BlockSpec((256, PART), lambda b: (0, 0)),
        ],
        out_shape=[
            jax.ShapeDtypeStruct((256, SW), jnp.bfloat16),
            jax.ShapeDtypeStruct((256, PART), jnp.float32),
        ],
        scratch_shapes=[pltpu.VMEM((256, SW), jnp.bfloat16)],
        compiler_params=pltpu.CompilerParams(vmem_limit_bytes=16 * MIB),
        cost_estimate=pl.CostEstimate(
            flops=2 * 256 * SW * 640, bytes_accessed=2 * MIB, transcendentals=0
        ),
    )(place, own, after, before, far_top, far_bottom, weight)


def shards(
    teacher_tokens,
    view_index,
    aug_embed,
    norm_gain,
    layer_scale,
    gate_weight,
    up_weight,
    down_weight,
    student_tokens,
    head_weight,
    owner,
):
    group, row, zl = lax.axis_index("group"), lax.axis_index("row"), lax.axis_index("zl")
    images = teacher_tokens.shape[0]
    place = jnp.stack([row, group, lax.axis_index("y"), lax.axis_index("x")]).astype(jnp.int32)

    down = jnp.concatenate(
        [
            down_weight[:, :1024],
            jnp.concatenate([down_weight[:16, 1024:], down_weight[16:, 1024:]], axis=1),
        ],
        axis=0,
    )
    block = jnp.concatenate([gate_weight, up_weight, down], axis=1)
    twin = lax.ppermute(block, ("group", "zl"), [(0, 1), (3, 2)])
    block = jnp.where(group == zl, block, twin)
    def collect(value, first):
        pieces = [value]
        for by in (-1, 2, 1):
            pairs = []
            for y in range(4):
                for x in range(4):
                    along_x = (y, (x + by) % 4)
                    along_y = ((y + by) % 4, x)
                    for core, (to_y, to_x) in enumerate(
                        (along_x, along_y) if first else (along_y, along_x)
                    ):
                        pairs.append((core * 16 + y * 4 + x, core * 16 + to_y * 4 + to_x))
            pieces.append(lax.ppermute(value, ("group", "y", "x"), pairs))
        return pieces

    line = gather(place, collect(block, True))
    weights_own = collect(line, False)
    both = lax.all_to_all(
        jnp.broadcast_to(line[None], (2,) + line.shape), "group", 0, 0, tiled=True
    )
    weights_other = [lax.dynamic_index_in_dim(both, 1 - group, 0, keepdims=False)]
    weights_other += [shift(piece, "group", 2, 1) for piece in weights_own[1:]]

    kinds = aug_embed.shape[0]
    kind_table = (
        view_index.reshape(-1)[:, None] == jnp.arange(kinds, dtype=jnp.int32)[None, :]
    ).astype(jnp.bfloat16)
    embedded = jnp.dot(kind_table, aug_embed, preferred_element_type=jnp.float32).reshape(
        images, 4, 1, PART
    )
    shifted = (teacher_tokens.astype(jnp.float32) + embedded).astype(jnp.bfloat16)
    residual = jnp.mean(shifted.astype(jnp.float32), axis=1).reshape(256, PART)
    quarters = [student_tokens[:, PART * c : PART * c + PART] for c in range(4)]
    own = jnp.concatenate(
        [
            shifted.reshape(2, 512, PART),
            jnp.stack([jnp.concatenate(quarters[:2]), jnp.concatenate(quarters[2:])]),
        ],
        axis=1,
    )
    own, twin = lax.optimization_barrier((own, twin))
    before = shift(own, "row", 4, 1)
    after = shift(own, "row", 4, -1)
    far_top = shift(before[0], "row", 4, 1)
    far_bottom = shift(after[1], "row", 4, -1)

    gain = norm_gain.astype(jnp.float32).reshape(1, D)
    normed = norm(place, own, after, before, far_top, far_bottom, gain)
    part, *away = branch(place, normed, weights_own, weights_other)
    held = (own, after, before, far_top, far_bottom)
    away, held = lax.optimization_barrier((away, held))
    got = [shift(away[j - 1], "row", 4, j) for j in (2, 1, 3)]
    pupils, head = student(place, *held, head_weight)

    averaged = part + sum(piece.astype(jnp.float32) for piece in got)
    target = (residual + layer_scale.astype(jnp.float32) * averaged).astype(jnp.bfloat16)
    target = target.astype(jnp.float32)
    sums = jnp.stack(
        [
            jnp.sum(head, axis=1),
            jnp.sum(head * head, axis=1),
            jnp.sum(target, axis=1),
            jnp.sum(head * target, axis=1),
            jnp.sum(target * target, axis=1),
        ]
    )
    sums = sums + sum(shift(sums, "row", 4, by) for by in (2, 1, 3))
    center = sums[0] / D
    spread = sums[1] / D - center * center
    scaler = lax.rsqrt(spread + 1e-05)
    pred_square = scaler * scaler * (sums[1] - D * center * center)
    pred_target = scaler * (sums[3] - center * sums[2])
    diff_square = pred_square - 2.0 * pred_target + sums[4]
    mean_first = -2.0 / IMAGES * sums[2] / D
    mean_second = 2.0 / IMAGES * (pred_square - pred_target) / D
    pred = (head - center[:, None]) * scaler[:, None]
    dpred = 2.0 / IMAGES * (pred - target)
    dz = (
        scaler[:, None] * (dpred - mean_first[:, None] - pred * mean_second[:, None])
    ).astype(jnp.bfloat16)
    errors = jnp.sum(diff_square.reshape(images, 8), axis=1) / (8 * D)
    mine = owner == jnp.arange(32, dtype=jnp.int32)[None, :]
    loss = jnp.sum(jnp.where(mine, errors[:, None], 0.0), axis=0)
    loss_high = loss.astype(jnp.bfloat16)
    loss_low = (loss - loss_high.astype(jnp.float32)).astype(jnp.bfloat16)

    grad = lax.dot_general(pupils, dz, (((0,), (0,)), ((), ())), preferred_element_type=jnp.float32)
    grad = grad.reshape(2, PART, PART)
    keep = lax.dynamic_index_in_dim(grad, group, 0, keepdims=False)
    give = lax.dynamic_index_in_dim(grad, 1 - group, 0, keepdims=False)
    half = keep + shift(give.astype(jnp.bfloat16), "group", 2, 1).astype(jnp.float32)
    half = half.astype(jnp.bfloat16).reshape(32, 12, PART)
    note = jnp.stack([loss_high, loss_low], axis=1)[:, :, None]
    note = jnp.broadcast_to(note, (32, 2, PART))
    packet = jnp.concatenate([half, note], axis=1)
    packet = lax.all_to_all(packet, COL, 0, 0, tiled=True).astype(jnp.float32)
    summed = jnp.sum(packet, axis=0)
    owner_loss = summed[12, :1] + summed[13, :1]
    piece = summed[:12].astype(jnp.bfloat16)
    piece = lax.all_to_all(jnp.broadcast_to(piece[None], (32, 12, PART)), COL, 0, 0, tiled=True)
    piece = piece.reshape(PART, PART)
    other = shift(piece, "group", 2, 1)
    head_grad = jnp.concatenate(
        [jnp.where(group == 0, piece, other), jnp.where(group == 0, other, piece)], axis=0
    ).astype(jnp.float32)
    return (head_grad, owner_loss)


def solution(mesh):
    fine = Mesh(mesh.devices.reshape(2, 4, 2, 4, 4), ("group", "row", "zl", "y", "x"))
    return jax.shard_map(
        shards,
        mesh=fine,
        in_specs=(
            P(EVERY, None, None, "row"),
            P(EVERY, None),
            P(None, "row"),
            P(),
            P("row"),
            P(COL, "row"),
            P(COL, "row"),
            P(("row",) + COL, None),
            P(EVERY, "row"),
            P(None, "row"),
            P(EVERY, None),
        ),
        out_specs=(P(None, "row"), P(EVERY)),
        check_vma=False,
    )
```

```python
import jax
import jax.numpy as jnp
from jax import lax
from jax.experimental import pallas as pl
from jax.experimental.pallas import tpu as pltpu
from jax.sharding import Mesh, PartitionSpec as P

D = 1536
SW = 768
PART = 384
YX = ("y", "x")
COL = ("zl", "y", "x")
EVERY = ("group", "zl", "y", "x")
IMAGES = 2048
MIB = 1024 * 1024


def shift(value, axis, size, by):
    return lax.ppermute(value, axis, [(i, (i + by) % size) for i in range(size)])


def norm_kernel(place, own, after, before, far_top, far_bottom, gain, out):
    row, group = place[0], place[1]
    far = jnp.where(pl.program_id(0) < 2, far_top[...], far_bottom[...])
    pieces = [own[0], after[0], far, before[0]]
    pieces = [piece.astype(jnp.float32) for piece in pieces]
    total = sum(jnp.sum(piece, axis=1, keepdims=True) for piece in pieces)
    mean = total * (1.0 / D)
    pieces = [piece - mean for piece in pieces]
    square = sum(jnp.sum(piece * piece, axis=1, keepdims=True) for piece in pieces)
    scale = lax.rsqrt(square * (1.0 / D) + 1e-06)
    for j, piece in enumerate(pieces):
        block = lax.rem(row + j, 4)
        source = pl.multiple_of(block * PART, PART)
        target = pl.multiple_of(lax.rem(block + 2 * group, 4) * PART, PART)
        value = piece * scale * gain[:, pl.ds(source, PART)]
        out[:, pl.ds(target, PART)] = value.astype(jnp.bfloat16)


def norm(place, own, after, before, far_top, far_bottom, gain):
    piece = pl.BlockSpec((1, 256, PART), lambda b: (b // 2, b % 2, 0))
    return pl.pallas_call(
        norm_kernel,
        grid=(4,),
        in_specs=[
            pl.BlockSpec(memory_space=pltpu.SMEM),
            piece,
            piece,
            piece,
            pl.BlockSpec((256, PART), lambda b: (jnp.minimum(b, 1), 0)),
            pl.BlockSpec((256, PART), lambda b: (jnp.maximum(b - 2, 0), 0)),
            pl.BlockSpec((1, D), lambda b: (0, 0)),
        ],
        out_specs=pl.BlockSpec((256, D), lambda b: (b, 0)),
        out_shape=jax.ShapeDtypeStruct((1024, D), jnp.bfloat16),
        compiler_params=pltpu.CompilerParams(vmem_limit_bytes=24 * MIB),
        cost_estimate=pl.CostEstimate(
            flops=30 * 10**9, bytes_accessed=4 * 1024 * D, transcendentals=0
        ),
    )(place, own, after, before, far_top, far_bottom, gain)


SPANS = (
    (0, 48, 0, 256, None),
    (0, 48, 1024, 256, None),
    (0, 48, 256, 768, None),
    (0, 48, 1280, 768, None),
    (0, 32, 2048, 1024, (0, 0)),
    (32, 16, 2048, 512, (0, 1024)),
    (32, 16, 2560, 512, (16, 1024)),
)


def branch_kernel(place, normed, *refs):
    row, group, y, x = place[0], place[1], place[2], place[3]
    sources = (refs[:4], refs[4:8])
    part, away1, away2, away3 = refs[8:12]
    weights, hidden, down, sems = refs[12:]

    def copy(side, k, span, along_y):
        top, height, start, width, spot = SPANS[span]
        columns = pl.ds(start, width)
        if spot is None:
            block, rows, target = weights.at[side], pl.ds(0, 48), columns
        else:
            block = down.at[side]
            rows, target = pl.ds(spot[0], height), pl.ds(spot[1], width)
        if along_y:
            block = block.at[lax.rem(y + k, 4), :, rows, target]
        else:
            block = block.at[:, lax.rem(x + k, 4), rows, target]
        source = sources[side][k].at[:, pl.ds(top, height), columns]
        return pltpu.make_async_copy(source, block, sems.at[side, k, span])

    def start_all(side, along_y, span):
        for k in range(4):
            copy(side, k, span, along_y).start()

    def wait_all(spans):
        for span in spans:
            for side in (0, 1):
                for k in range(4):
                    copy(side, k, span, True).wait()

    for span in range(7):
        for side in (0, 1):
            along = group == side

            @pl.when(along)
            def _():
                start_all(side, True, span)

            @pl.when(jnp.logical_not(along))
            def _():
                start_all(side, False, span)

    def project(kind, n):
        start = kind * 1024 + n * 256
        return sum(
            jnp.dot(
                normed[:, 768 * side : 768 * side + 768],
                weights[side, :, :, :, start : start + 256].reshape(768, 256),
                preferred_element_type=jnp.float32,
            )
            for side in (0, 1)
        )

    for n in range(4):
        if n == 0:
            wait_all((0, 1))
        if n == 1:
            wait_all((2, 3))
        gate = project(0, n)
        upward = project(1, n)
        value = gate * upward / (1.0 + jnp.exp(-gate))
        value = jnp.sum(value.reshape(32, 4, 8, 256), axis=1).reshape(256, 256) * 0.25
        target = pl.multiple_of(lax.rem(n + 2 * group, 4) * 256, 256)
        hidden[:, pl.ds(target, 256)] = value.astype(jnp.bfloat16)

    wait_all((4, 5, 6))
    for j, out in ((2, away2), (1, away1), (3, away3), (0, part)):
        start = pl.multiple_of(lax.rem(row + j, 4) * PART, PART)
        value = jnp.dot(
            hidden[...],
            down[:, :, :, :, pl.ds(start, PART)].reshape(1024, PART),
            preferred_element_type=jnp.float32,
        )
        out[...] = value.astype(out.dtype)


def branch(place, normed, own, other):
    narrow = jax.ShapeDtypeStruct((256, PART), jnp.bfloat16)
    vmem = pl.BlockSpec(memory_space=pltpu.VMEM)
    return pl.pallas_call(
        branch_kernel,
        in_specs=[pl.BlockSpec(memory_space=pltpu.SMEM), vmem]
        + [pl.BlockSpec(memory_space=pl.ANY)] * 8,
        out_specs=[vmem] * 4,
        out_shape=[jax.ShapeDtypeStruct((256, PART), jnp.float32), narrow, narrow, narrow],
        scratch_shapes=[
            pltpu.VMEM((2, 4, 4, 48, 2048), jnp.bfloat16),
            pltpu.VMEM((256, 1024), jnp.bfloat16),
            pltpu.VMEM((2, 4, 4, 32, D), jnp.bfloat16),
            pltpu.SemaphoreType.DMA((2, 4, 7)),
        ],
        compiler_params=pltpu.CompilerParams(vmem_limit_bytes=40 * MIB),
        cost_estimate=pl.CostEstimate(
            flops=2 * 1024 * D * 2048, bytes_accessed=10 * MIB, transcendentals=1024 * 1024
        ),
    )(place, normed, *own, *other)


def gather_kernel(place, *refs):
    sources, out = refs[:4], refs[4]
    position = jnp.where(place[1] == 0, place[3], place[2])
    for k, source in enumerate(sources):
        out[lax.rem(position + k, 4)] = source[...]


def gather(place, blocks):
    vmem = pl.BlockSpec(memory_space=pltpu.VMEM)
    return pl.pallas_call(
        gather_kernel,
        in_specs=[pl.BlockSpec(memory_space=pltpu.SMEM)] + [vmem] * 4,
        out_specs=vmem,
        out_shape=jax.ShapeDtypeStruct((4,) + blocks[0].shape, jnp.bfloat16),
        compiler_params=pltpu.CompilerParams(vmem_limit_bytes=16 * MIB),
        cost_estimate=pl.CostEstimate(flops=0, bytes_accessed=3 * MIB, transcendentals=0),
    )(place, *blocks)


def student_kernel(place, own, after, before, far_top, far_bottom, weight, pupils, head, gathered):
    row = place[0]
    pieces = (
        (own[0], own[1]),
        (after[0], after[1]),
        (far_top[...], far_bottom[...]),
        (before[0], before[1]),
    )
    for j, piece in enumerate(pieces):
        for i, half in enumerate(piece):
            rows = (2 * j + i) * 32
            gathered[rows : rows + 32, 0:PART] = half[0:32]
            gathered[rows : rows + 32, PART:SW] = half[32:64]
    target = lax.broadcasted_iota(jnp.int32, (256, 256), 0)
    source = lax.broadcasted_iota(jnp.int32, (256, 256), 1)
    image, patch = target // 8, lax.rem(target, 8)
    place_of = lax.rem(patch - 2 * row + 8, 8) * 32 + image
    order = jnp.where(source == place_of, 1.0, 0.0).astype(jnp.bfloat16)
    value = jnp.dot(order, gathered[...], preferred_element_type=jnp.float32)
    value = value.astype(jnp.bfloat16)
    pupils[...] = value
    head[...] = jnp.dot(value, weight[...], preferred_element_type=jnp.float32)


def student(place, own, after, before, far_top, far_bottom, weight):
    piece = pl.BlockSpec((2, 64, PART), lambda b: (0, 8, 0))
    half = pl.BlockSpec((64, PART), lambda b: (8, 0))
    return pl.pallas_call(
        student_kernel,
        grid=(1,),
        in_specs=[
            pl.BlockSpec(memory_space=pltpu.SMEM),
            piece,
            piece,
            piece,
            half,
            half,
            pl.BlockSpec((SW, PART), lambda b: (0, 0)),
        ],
        out_specs=[
            pl.BlockSpec((256, SW), lambda b: (0, 0)),
            pl.BlockSpec((256, PART), lambda b: (0, 0)),
        ],
        out_shape=[
            jax.ShapeDtypeStruct((256, SW), jnp.bfloat16),
            jax.ShapeDtypeStruct((256, PART), jnp.float32),
        ],
        scratch_shapes=[pltpu.VMEM((256, SW), jnp.bfloat16)],
        compiler_params=pltpu.CompilerParams(vmem_limit_bytes=16 * MIB),
        cost_estimate=pl.CostEstimate(
            flops=2 * 256 * SW * 640, bytes_accessed=2 * MIB, transcendentals=0
        ),
    )(place, own, after, before, far_top, far_bottom, weight)


def pack_kernel(gate, up, down, out, sems):
    copies = [
        pltpu.make_async_copy(gate, out.at[:, 0:1024], sems.at[0]),
        pltpu.make_async_copy(up, out.at[:, 1024:2048], sems.at[1]),
        pltpu.make_async_copy(down.at[:, 0:1024], out.at[0:32, 2048:3072], sems.at[2]),
        pltpu.make_async_copy(
            down.at[0:16, 1024:1536], out.at[32:48, 2048:2560], sems.at[3]
        ),
        pltpu.make_async_copy(
            down.at[16:32, 1024:1536], out.at[32:48, 2560:3072], sems.at[4]
        ),
    ]
    for copy in copies:
        copy.start()
    for copy in copies:
        copy.wait()


def pack(gate, up, down):
    return pl.pallas_call(
        pack_kernel,
        in_specs=[pl.BlockSpec(memory_space=pl.ANY)] * 3,
        out_specs=pl.BlockSpec(memory_space=pltpu.VMEM),
        out_shape=jax.ShapeDtypeStruct((48, 3072), jnp.bfloat16),
        scratch_shapes=[pltpu.SemaphoreType.DMA((5,))],
        compiler_params=pltpu.CompilerParams(vmem_limit_bytes=56 * MIB),
        cost_estimate=pl.CostEstimate(flops=0, bytes_accessed=MIB, transcendentals=0),
    )(gate, up, down)


def shards(
    teacher_tokens,
    view_index,
    aug_embed,
    norm_gain,
    layer_scale,
    gate_weight,
    up_weight,
    down_weight,
    student_tokens,
    head_weight,
    owner,
):
    group, row, zl = lax.axis_index("group"), lax.axis_index("row"), lax.axis_index("zl")
    images = teacher_tokens.shape[0]
    place = jnp.stack([row, group, lax.axis_index("y"), lax.axis_index("x")]).astype(jnp.int32)

    block = pack(gate_weight, up_weight, down_weight)
    twin = lax.ppermute(block, ("group", "zl"), [(0, 1), (3, 2)])
    block = jnp.where(group == zl, block, twin)
    def collect(value, first):
        pieces = [value]
        for by in (-1, 2, 1):
            pairs = []
            for y in range(4):
                for x in range(4):
                    along_x = (y, (x + by) % 4)
                    along_y = ((y + by) % 4, x)
                    for core, (to_y, to_x) in enumerate(
                        (along_x, along_y) if first else (along_y, along_x)
                    ):
                        pairs.append((core * 16 + y * 4 + x, core * 16 + to_y * 4 + to_x))
            pieces.append(lax.ppermute(value, ("group", "y", "x"), pairs))
        return pieces

    line = gather(place, collect(block, True))
    weights_own = collect(line, False)
    both = lax.all_to_all(
        jnp.broadcast_to(line[None], (2,) + line.shape), "group", 0, 0, tiled=True
    )
    weights_other = [lax.dynamic_index_in_dim(both, 1 - group, 0, keepdims=False)]
    weights_other += [shift(piece, "group", 2, 1) for piece in weights_own[1:]]

    kinds = aug_embed.shape[0]
    kind_table = (
        view_index.reshape(-1)[:, None] == jnp.arange(kinds, dtype=jnp.int32)[None, :]
    ).astype(jnp.bfloat16)
    embedded = jnp.dot(kind_table, aug_embed, preferred_element_type=jnp.float32).reshape(
        images, 4, 1, PART
    )
    shifted = (teacher_tokens.astype(jnp.float32) + embedded).astype(jnp.bfloat16)
    residual = jnp.mean(shifted.astype(jnp.float32), axis=1).reshape(256, PART)
    quarters = [student_tokens[:, PART * c : PART * c + PART] for c in range(4)]
    own = jnp.concatenate(
        [
            shifted.reshape(2, 512, PART),
            jnp.stack([jnp.concatenate(quarters[:2]), jnp.concatenate(quarters[2:])]),
        ],
        axis=1,
    )
    own, twin = lax.optimization_barrier((own, twin))
    before = shift(own, "row", 4, 1)
    after = shift(own, "row", 4, -1)
    far_top = shift(before[0], "row", 4, 1)
    far_bottom = shift(after[1], "row", 4, -1)

    gain = norm_gain.astype(jnp.float32).reshape(1, D)
    normed = norm(place, own, after, before, far_top, far_bottom, gain)
    part, *away = branch(place, normed, weights_own, weights_other)
    held = (own, after, before, far_top, far_bottom)
    away, held = lax.optimization_barrier((away, held))
    got = [shift(away[j - 1], "row", 4, j) for j in (2, 1, 3)]
    pupils, head = student(place, *held, head_weight)

    averaged = part + sum(piece.astype(jnp.float32) for piece in got)
    target = (residual + layer_scale.astype(jnp.float32) * averaged).astype(jnp.bfloat16)
    target = target.astype(jnp.float32)
    sums = jnp.stack(
        [
            jnp.sum(head, axis=1),
            jnp.sum(head * head, axis=1),
            jnp.sum(target, axis=1),
            jnp.sum(head * target, axis=1),
            jnp.sum(target * target, axis=1),
        ]
    )
    sums = sums + sum(shift(sums, "row", 4, by) for by in (2, 1, 3))
    center = sums[0] / D
    spread = sums[1] / D - center * center
    scaler = lax.rsqrt(spread + 1e-05)
    pred_square = scaler * scaler * (sums[1] - D * center * center)
    pred_target = scaler * (sums[3] - center * sums[2])
    diff_square = pred_square - 2.0 * pred_target + sums[4]
    mean_first = -2.0 / IMAGES * sums[2] / D
    mean_second = 2.0 / IMAGES * (pred_square - pred_target) / D
    pred = (head - center[:, None]) * scaler[:, None]
    dpred = 2.0 / IMAGES * (pred - target)
    dz = (
        scaler[:, None] * (dpred - mean_first[:, None] - pred * mean_second[:, None])
    ).astype(jnp.bfloat16)
    errors = jnp.sum(diff_square.reshape(images, 8), axis=1) / (8 * D)
    mine = owner == jnp.arange(32, dtype=jnp.int32)[None, :]
    loss = jnp.sum(jnp.where(mine, errors[:, None], 0.0), axis=0)
    loss_high = loss.astype(jnp.bfloat16)
    loss_low = (loss - loss_high.astype(jnp.float32)).astype(jnp.bfloat16)

    grad = lax.dot_general(pupils, dz, (((0,), (0,)), ((), ())), preferred_element_type=jnp.float32)
    grad = grad.reshape(2, PART, PART)
    keep = lax.dynamic_index_in_dim(grad, group, 0, keepdims=False)
    give = lax.dynamic_index_in_dim(grad, 1 - group, 0, keepdims=False)
    half = keep + shift(give.astype(jnp.bfloat16), "group", 2, 1).astype(jnp.float32)
    half = half.astype(jnp.bfloat16).reshape(32, 12, PART)
    note = jnp.stack([loss_high, loss_low], axis=1)[:, :, None]
    note = jnp.broadcast_to(note, (32, 2, PART))
    packet = jnp.concatenate([half, note], axis=1)
    packet = lax.all_to_all(packet, COL, 0, 0, tiled=True).astype(jnp.float32)
    summed = jnp.sum(packet, axis=0)
    owner_loss = summed[12, :1] + summed[13, :1]
    piece = summed[:12].astype(jnp.bfloat16)
    piece = lax.all_to_all(jnp.broadcast_to(piece[None], (32, 12, PART)), COL, 0, 0, tiled=True)
    piece = piece.reshape(PART, PART)
    other = shift(piece, "group", 2, 1)
    head_grad = jnp.concatenate(
        [jnp.where(group == 0, piece, other), jnp.where(group == 0, other, piece)], axis=0
    ).astype(jnp.float32)
    return (head_grad, owner_loss)


def solution(mesh):
    fine = Mesh(mesh.devices.reshape(2, 4, 2, 4, 4), ("group", "row", "zl", "y", "x"))
    return jax.shard_map(
        shards,
        mesh=fine,
        in_specs=(
            P(EVERY, None, None, "row"),
            P(EVERY, None),
            P(None, "row"),
            P(),
            P("row"),
            P(COL, "row"),
            P(COL, "row"),
            P(("row",) + COL, None),
            P(EVERY, "row"),
            P(None, "row"),
            P(EVERY, None),
        ),
        out_specs=(P(None, "row"), P(EVERY)),
        check_vma=False,
    )
```

```python
import jax
import jax.numpy as jnp
from jax import lax
from jax.experimental import pallas as pl
from jax.experimental.pallas import tpu as pltpu
from jax.sharding import Mesh, PartitionSpec as P

D = 1536
SW = 768
PART = 384
YX = ("y", "x")
COL = ("zl", "y", "x")
EVERY = ("group", "zl", "y", "x")
IMAGES = 2048
MIB = 1024 * 1024


def shift(value, axis, size, by):
    return lax.ppermute(value, axis, [(i, (i + by) % size) for i in range(size)])


def norm_kernel(place, own, after, before, far_top, far_bottom, gain, out):
    row, group = place[0], place[1]
    far = jnp.where(pl.program_id(0) < 2, far_top[...], far_bottom[...])
    pieces = [own[0], after[0], far, before[0]]
    pieces = [piece.astype(jnp.float32) for piece in pieces]
    total = sum(jnp.sum(piece, axis=1, keepdims=True) for piece in pieces)
    mean = total * (1.0 / D)
    pieces = [piece - mean for piece in pieces]
    square = sum(jnp.sum(piece * piece, axis=1, keepdims=True) for piece in pieces)
    scale = lax.rsqrt(square * (1.0 / D) + 1e-06)
    for j, piece in enumerate(pieces):
        block = lax.rem(row + j, 4)
        source = pl.multiple_of(block * PART, PART)
        target = pl.multiple_of(lax.rem(block + 2 * group, 4) * PART, PART)
        value = piece * scale * gain[:, pl.ds(source, PART)]
        out[:, pl.ds(target, PART)] = value.astype(jnp.bfloat16)


def norm(place, own, after, before, far_top, far_bottom, gain):
    piece = pl.BlockSpec((1, 256, PART), lambda b: (b // 2, b % 2, 0))
    return pl.pallas_call(
        norm_kernel,
        grid=(4,),
        in_specs=[
            pl.BlockSpec(memory_space=pltpu.SMEM),
            piece,
            piece,
            piece,
            pl.BlockSpec((256, PART), lambda b: (jnp.minimum(b, 1), 0)),
            pl.BlockSpec((256, PART), lambda b: (jnp.maximum(b - 2, 0), 0)),
            pl.BlockSpec((1, D), lambda b: (0, 0)),
        ],
        out_specs=pl.BlockSpec((256, D), lambda b: (b, 0)),
        out_shape=jax.ShapeDtypeStruct((1024, D), jnp.bfloat16),
        compiler_params=pltpu.CompilerParams(vmem_limit_bytes=24 * MIB),
        cost_estimate=pl.CostEstimate(
            flops=30 * 10**9, bytes_accessed=4 * 1024 * D, transcendentals=0
        ),
    )(place, own, after, before, far_top, far_bottom, gain)


SPANS = (
    (0, 48, 0, 256, None),
    (0, 48, 1024, 256, None),
    (0, 48, 256, 768, None),
    (0, 48, 1280, 768, None),
    (0, 32, 2048, 1024, (0, 0)),
    (32, 16, 2048, 512, (0, 1024)),
    (32, 16, 2560, 512, (16, 1024)),
)


def branch_kernel(place, normed, *refs):
    row, group, y, x = place[0], place[1], place[2], place[3]
    sources = (refs[:4], refs[4:8])
    part, away1, away2, away3 = refs[8:12]
    weights, hidden, down, sems = refs[12:]

    def copy(side, k, span, along_y):
        top, height, start, width, spot = SPANS[span]
        columns = pl.ds(start, width)
        if spot is None:
            block, rows, target = weights.at[side], pl.ds(0, 48), columns
        else:
            block = down.at[side]
            rows, target = pl.ds(spot[0], height), pl.ds(spot[1], width)
        if along_y:
            block = block.at[lax.rem(y + k, 4), :, rows, target]
        else:
            block = block.at[:, lax.rem(x + k, 4), rows, target]
        source = sources[side][k].at[:, pl.ds(top, height), columns]
        return pltpu.make_async_copy(source, block, sems.at[side, k, span])

    def start_all(side, along_y, span):
        for k in range(4):
            copy(side, k, span, along_y).start()

    def wait_all(spans):
        for span in spans:
            for side in (0, 1):
                for k in range(4):
                    copy(side, k, span, True).wait()

    for span in range(7):
        for side in (0, 1):
            along = group == side

            @pl.when(along)
            def _():
                start_all(side, True, span)

            @pl.when(jnp.logical_not(along))
            def _():
                start_all(side, False, span)

    def project(kind, n):
        start = kind * 1024 + n * 256
        return sum(
            jnp.dot(
                normed[:, 768 * side : 768 * side + 768],
                weights[side, :, :, :, start : start + 256].reshape(768, 256),
                preferred_element_type=jnp.float32,
            )
            for side in (0, 1)
        )

    for n in range(4):
        if n == 0:
            wait_all((0, 1))
        if n == 1:
            wait_all((2, 3))
        gate = project(0, n)
        upward = project(1, n)
        value = gate * upward / (1.0 + jnp.exp(-gate))
        value = jnp.sum(value.reshape(32, 4, 8, 256), axis=1).reshape(256, 256) * 0.25
        target = pl.multiple_of(lax.rem(n + 2 * group, 4) * 256, 256)
        hidden[:, pl.ds(target, 256)] = value.astype(jnp.bfloat16)

    wait_all((4, 5, 6))
    for j, out in ((2, away2), (1, away1), (3, away3), (0, part)):
        start = pl.multiple_of(lax.rem(row + j, 4) * PART, PART)
        value = jnp.dot(
            hidden[...],
            down[:, :, :, :, pl.ds(start, PART)].reshape(1024, PART),
            preferred_element_type=jnp.float32,
        )
        out[...] = value.astype(out.dtype)


def branch(place, normed, own, other):
    narrow = jax.ShapeDtypeStruct((256, PART), jnp.bfloat16)
    vmem = pl.BlockSpec(memory_space=pltpu.VMEM)
    return pl.pallas_call(
        branch_kernel,
        in_specs=[pl.BlockSpec(memory_space=pltpu.SMEM), vmem]
        + [pl.BlockSpec(memory_space=pl.ANY)] * 8,
        out_specs=[vmem] * 4,
        out_shape=[jax.ShapeDtypeStruct((256, PART), jnp.float32), narrow, narrow, narrow],
        scratch_shapes=[
            pltpu.VMEM((2, 4, 4, 48, 2048), jnp.bfloat16),
            pltpu.VMEM((256, 1024), jnp.bfloat16),
            pltpu.VMEM((2, 4, 4, 32, D), jnp.bfloat16),
            pltpu.SemaphoreType.DMA((2, 4, 7)),
        ],
        compiler_params=pltpu.CompilerParams(vmem_limit_bytes=40 * MIB),
        cost_estimate=pl.CostEstimate(
            flops=2 * 1024 * D * 2048, bytes_accessed=10 * MIB, transcendentals=1024 * 1024
        ),
    )(place, normed, *own, *other)


def gather_kernel(place, *refs):
    sources, out = refs[:4], refs[4]
    position = jnp.where(place[1] == 0, place[3], place[2])
    for k, source in enumerate(sources):
        out[lax.rem(position + k, 4)] = source[...]


def gather(place, blocks):
    vmem = pl.BlockSpec(memory_space=pltpu.VMEM)
    return pl.pallas_call(
        gather_kernel,
        in_specs=[pl.BlockSpec(memory_space=pltpu.SMEM)] + [vmem] * 4,
        out_specs=vmem,
        out_shape=jax.ShapeDtypeStruct((4,) + blocks[0].shape, jnp.bfloat16),
        compiler_params=pltpu.CompilerParams(vmem_limit_bytes=16 * MIB),
        cost_estimate=pl.CostEstimate(flops=0, bytes_accessed=3 * MIB, transcendentals=0),
    )(place, *blocks)


def student_kernel(place, own, after, before, far_top, far_bottom, weight, pupils, head, gathered):
    row = place[0]
    pieces = (
        (own[0], own[1]),
        (after[0], after[1]),
        (far_top[...], far_bottom[...]),
        (before[0], before[1]),
    )
    for j, piece in enumerate(pieces):
        for i, half in enumerate(piece):
            rows = (2 * j + i) * 32
            gathered[rows : rows + 32, 0:PART] = half[0:32]
            gathered[rows : rows + 32, PART:SW] = half[32:64]
    target = lax.broadcasted_iota(jnp.int32, (256, 256), 0)
    source = lax.broadcasted_iota(jnp.int32, (256, 256), 1)
    image, patch = target // 8, lax.rem(target, 8)
    place_of = lax.rem(patch - 2 * row + 8, 8) * 32 + image
    order = jnp.where(source == place_of, 1.0, 0.0).astype(jnp.bfloat16)
    value = jnp.dot(order, gathered[...], preferred_element_type=jnp.float32)
    value = value.astype(jnp.bfloat16)
    pupils[...] = value
    head[...] = jnp.dot(value, weight[...], preferred_element_type=jnp.float32)


def student(place, own, after, before, far_top, far_bottom, weight):
    piece = pl.BlockSpec((2, 64, PART), lambda b: (0, 8, 0))
    half = pl.BlockSpec((64, PART), lambda b: (8, 0))
    return pl.pallas_call(
        student_kernel,
        grid=(1,),
        in_specs=[
            pl.BlockSpec(memory_space=pltpu.SMEM),
            piece,
            piece,
            piece,
            half,
            half,
            pl.BlockSpec((SW, PART), lambda b: (0, 0)),
        ],
        out_specs=[
            pl.BlockSpec((256, SW), lambda b: (0, 0)),
            pl.BlockSpec((256, PART), lambda b: (0, 0)),
        ],
        out_shape=[
            jax.ShapeDtypeStruct((256, SW), jnp.bfloat16),
            jax.ShapeDtypeStruct((256, PART), jnp.float32),
        ],
        scratch_shapes=[pltpu.VMEM((256, SW), jnp.bfloat16)],
        compiler_params=pltpu.CompilerParams(vmem_limit_bytes=16 * MIB),
        cost_estimate=pl.CostEstimate(
            flops=2 * 256 * SW * 640, bytes_accessed=2 * MIB, transcendentals=0
        ),
    )(place, own, after, before, far_top, far_bottom, weight)


def pack_kernel(gate, up, down, out, sems):
    copies = [
        pltpu.make_async_copy(gate, out.at[:, 0:1024], sems.at[0]),
        pltpu.make_async_copy(up, out.at[:, 1024:2048], sems.at[1]),
        pltpu.make_async_copy(down.at[:, 0:1024], out.at[0:32, 2048:3072], sems.at[2]),
        pltpu.make_async_copy(
            down.at[0:16, 1024:1536], out.at[32:48, 2048:2560], sems.at[3]
        ),
        pltpu.make_async_copy(
            down.at[16:32, 1024:1536], out.at[32:48, 2560:3072], sems.at[4]
        ),
    ]
    for copy in copies:
        copy.start()
    for copy in copies:
        copy.wait()


def pack(gate, up, down):
    return pl.pallas_call(
        pack_kernel,
        in_specs=[pl.BlockSpec(memory_space=pl.ANY)] * 3,
        out_specs=pl.BlockSpec(memory_space=pltpu.VMEM),
        out_shape=jax.ShapeDtypeStruct((48, 3072), jnp.bfloat16),
        scratch_shapes=[pltpu.SemaphoreType.DMA((5,))],
        compiler_params=pltpu.CompilerParams(vmem_limit_bytes=56 * MIB),
        cost_estimate=pl.CostEstimate(flops=0, bytes_accessed=MIB, transcendentals=0),
    )(gate, up, down)


def shards(
    teacher_tokens,
    view_index,
    aug_embed,
    norm_gain,
    layer_scale,
    gate_weight,
    up_weight,
    down_weight,
    student_tokens,
    head_weight,
    owner,
):
    group, row, zl = lax.axis_index("group"), lax.axis_index("row"), lax.axis_index("zl")
    images = teacher_tokens.shape[0]
    place = jnp.stack([row, group, lax.axis_index("y"), lax.axis_index("x")]).astype(jnp.int32)

    block = pack(gate_weight, up_weight, down_weight)
    twin = lax.ppermute(block, ("group", "zl"), [(0, 1), (3, 2)])
    block = jnp.where(group == zl, block, twin)
    def collect(value, first):
        pieces = [value]
        for by in (-1, 2, 1):
            pairs = []
            for y in range(4):
                for x in range(4):
                    along_x = (y, (x + by) % 4)
                    along_y = ((y + by) % 4, x)
                    for core, (to_y, to_x) in enumerate(
                        (along_x, along_y) if first else (along_y, along_x)
                    ):
                        pairs.append((core * 16 + y * 4 + x, core * 16 + to_y * 4 + to_x))
            pieces.append(lax.ppermute(value, ("group", "y", "x"), pairs))
        return pieces

    line = gather(place, collect(block, True))
    weights_own = collect(line, False)
    both = lax.all_to_all(
        jnp.broadcast_to(line[None], (2,) + line.shape), "group", 0, 0, tiled=True
    )
    weights_other = [lax.dynamic_index_in_dim(both, 1 - group, 0, keepdims=False)]
    weights_other += [shift(piece, "group", 2, 1) for piece in weights_own[1:]]

    kinds = aug_embed.shape[0]
    kind_table = (
        view_index.reshape(-1)[:, None] == jnp.arange(kinds, dtype=jnp.int32)[None, :]
    ).astype(jnp.bfloat16)
    embedded = jnp.dot(kind_table, aug_embed, preferred_element_type=jnp.float32).reshape(
        images, 4, 1, PART
    )
    shifted = (teacher_tokens.astype(jnp.float32) + embedded).astype(jnp.bfloat16)
    residual = jnp.mean(shifted.astype(jnp.float32), axis=1).reshape(256, PART)
    quarters = [student_tokens[:, PART * c : PART * c + PART] for c in range(4)]
    own = jnp.concatenate(
        [
            shifted.reshape(2, 512, PART),
            jnp.stack([jnp.concatenate(quarters[:2]), jnp.concatenate(quarters[2:])]),
        ],
        axis=1,
    )
    own, twin = lax.optimization_barrier((own, twin))
    before = shift(own, "row", 4, 1)
    after = shift(own, "row", 4, -1)
    far_top = shift(before[0], "row", 4, 1)
    far_bottom = shift(after[1], "row", 4, -1)

    gain = norm_gain.astype(jnp.float32).reshape(1, D)
    normed = norm(place, own, after, before, far_top, far_bottom, gain)
    part, *away = branch(place, normed, weights_own, weights_other)
    held = (own, after, before, far_top, far_bottom)
    away, held = lax.optimization_barrier((away, held))
    got = [shift(away[j - 1], "row", 4, j) for j in (1, 3, 2)]
    pupils, head = student(place, *held, head_weight)

    averaged = part + sum(piece.astype(jnp.float32) for piece in got)
    target = (residual + layer_scale.astype(jnp.float32) * averaged).astype(jnp.bfloat16)
    target = target.astype(jnp.float32)
    sums = jnp.stack(
        [
            jnp.sum(head, axis=1),
            jnp.sum(head * head, axis=1),
            jnp.sum(target, axis=1),
            jnp.sum(head * target, axis=1),
            jnp.sum(target * target, axis=1),
        ]
    )
    sums = sums + sum(shift(sums, "row", 4, by) for by in (2, 1, 3))
    center = sums[0] / D
    spread = sums[1] / D - center * center
    scaler = lax.rsqrt(spread + 1e-05)
    pred_square = scaler * scaler * (sums[1] - D * center * center)
    pred_target = scaler * (sums[3] - center * sums[2])
    diff_square = pred_square - 2.0 * pred_target + sums[4]
    mean_first = -2.0 / IMAGES * sums[2] / D
    mean_second = 2.0 / IMAGES * (pred_square - pred_target) / D
    pred = (head - center[:, None]) * scaler[:, None]
    dpred = 2.0 / IMAGES * (pred - target)
    dz = (
        scaler[:, None] * (dpred - mean_first[:, None] - pred * mean_second[:, None])
    ).astype(jnp.bfloat16)
    errors = jnp.sum(diff_square.reshape(images, 8), axis=1) / (8 * D)
    mine = owner == jnp.arange(32, dtype=jnp.int32)[None, :]
    loss = jnp.sum(jnp.where(mine, errors[:, None], 0.0), axis=0)
    loss_high = loss.astype(jnp.bfloat16)
    loss_low = (loss - loss_high.astype(jnp.float32)).astype(jnp.bfloat16)

    grad = lax.dot_general(pupils, dz, (((0,), (0,)), ((), ())), preferred_element_type=jnp.float32)
    grad = grad.reshape(2, PART, PART)
    keep = lax.dynamic_index_in_dim(grad, group, 0, keepdims=False)
    give = lax.dynamic_index_in_dim(grad, 1 - group, 0, keepdims=False)
    half = keep + shift(give.astype(jnp.bfloat16), "group", 2, 1).astype(jnp.float32)
    half = half.astype(jnp.bfloat16).reshape(32, 12, PART)
    note = jnp.stack([loss_high, loss_low], axis=1)[:, :, None]
    note = jnp.broadcast_to(note, (32, 2, PART))
    packet = jnp.concatenate([half, note], axis=1)
    packet = lax.all_to_all(packet, COL, 0, 0, tiled=True).astype(jnp.float32)
    summed = jnp.sum(packet, axis=0)
    owner_loss = summed[12, :1] + summed[13, :1]
    piece = summed[:12].astype(jnp.bfloat16)
    piece = lax.all_to_all(jnp.broadcast_to(piece[None], (32, 12, PART)), COL, 0, 0, tiled=True)
    piece = piece.reshape(PART, PART)
    other = shift(piece, "group", 2, 1)
    head_grad = jnp.concatenate(
        [jnp.where(group == 0, piece, other), jnp.where(group == 0, other, piece)], axis=0
    ).astype(jnp.float32)
    return (head_grad, owner_loss)


def solution(mesh):
    fine = Mesh(mesh.devices.reshape(2, 4, 2, 4, 4), ("group", "row", "zl", "y", "x"))
    return jax.shard_map(
        shards,
        mesh=fine,
        in_specs=(
            P(EVERY, None, None, "row"),
            P(EVERY, None),
            P(None, "row"),
            P(),
            P("row"),
            P(COL, "row"),
            P(COL, "row"),
            P(("row",) + COL, None),
            P(EVERY, "row"),
            P(None, "row"),
            P(EVERY, None),
        ),
        out_specs=(P(None, "row"), P(EVERY)),
        check_vma=False,
    )
```
